32 devices in a mesh: outer: 4 (over x, core), inner: 8 (over z, y).
Axes of the slice: x: 2, y: 2, z: 4, core: 2. Of those that a mesh axis runs over, the one named last changes fastest.
Arguments:
- projected: bfloat16 [4096, 12288], P(('outer', 'inner')), may hold values from -6 to 6
- short_filter: bfloat16 [3, 12288], replicated, may hold values from -3.5 to 3.5
- long_filter: bfloat16 [4096, 4096], P(('outer', 'inner')), may hold values from 0 to 0.35
- skip: float32 [4096], replicated, may hold values from 0.1 to 1.9
Outputs:
- mixed: bfloat16 [4096, 4096], P(('outer', 'inner'))
The draws below stay inside these ranges and needn't reach their ends.
All inputs are finite; a program needn't handle non-finite values.
Results may differ from the reference program's by a relative error of at most 0.0075.
Values may be sent and summed in bfloat16 or wider, within the bound.
A program may use at most 128 MiB of HBM per device.

```python
import math
import jax
import jax.numpy as jnp
from jax import lax

C = 4096
SHORT = 3
TOK_DEV = 128
SEQ = 4096
BLOCKS = 64
TRANSFORM = 8192
N_OUTER = 4
N_INNER = 8


def draw_long_filter(key, part):
    keys = jax.random.split(key, 6)
    slow_share = 0.5
    lower_rough = 0.5
    upper_rough = 1.5
    slow_mask = jax.random.uniform(keys[0], (C,)) < slow_share
    slow_log = jax.random.uniform(keys[1], (C,), minval=math.log(0.5 / SEQ), maxval=math.log(2.0 / SEQ))
    fast_log = jax.random.uniform(keys[2], (C,), minval=math.log(1.0 / 400.0), maxval=math.log(1.0 / 30.0))
    decay_rate = jnp.exp(jnp.where(slow_mask, slow_log, fast_log))
    lag_index = jnp.arange(SEQ, dtype=jnp.int32)[:, None]
    positions = lag_index.astype(jnp.float32)
    roughness = jax.random.uniform(keys[3], (SEQ, C), minval=lower_rough, maxval=upper_rough)
    echo_rough = jax.random.uniform(keys[4], (SEQ, C), minval=lower_rough, maxval=upper_rough)
    delay = jax.random.randint(keys[5], (C,), SEQ // 8, SEQ // 2 + 1).astype(jnp.int32)
    main_part = jnp.sqrt(decay_rate)[None, :] * jnp.exp(-decay_rate[None, :] * positions) * roughness
    since_delay = jnp.maximum(lag_index - delay[None, :], 0).astype(jnp.float32)
    echo_live = jnp.logical_and(lag_index >= delay[None, :], jnp.logical_not(slow_mask)[None, :])
    echo_part = 0.5 * jnp.sqrt(decay_rate)[None, :] * jnp.exp(-decay_rate[None, :] * since_delay) * echo_rough
    filter_taps = main_part + jnp.where(echo_live, echo_part, 0.0)
    return filter_taps.astype(jnp.bfloat16)


def block_scale(stream_key, extent, cuts, smallest, largest):
    loudness, own = 1.0, jax.random.fold_in(stream_key, 6)
    for dim, shards_of in cuts:
        draws = jnp.exp(jax.random.uniform(jax.random.fold_in(own, dim), (shards_of,), jnp.float32, smallest / len(cuts), largest / len(cuts)))
        loudness = loudness * jnp.repeat(draws, extent[dim] // shards_of).reshape([-1 if axis == dim else 1 for axis in range(len(extent))])
    return loudness


def gaussian(stream_key, shape, scale, most, cuts=(), held_as=jnp.bfloat16):
    result = scale * jax.random.normal(stream_key, shape, jnp.float32)
    if cuts:
        result = result * block_scale(stream_key, shape, cuts, -0.22, 0.18)
    return jnp.clip(result, -most, most).astype(held_as)


def setup_inputs(seed: int = 0) -> dict:
    splits = jax.random.split(jax.random.key(seed), 5)
    return {
        "projected": gaussian(splits[0], (SEQ, 3 * C), 1.0, 6.0, ((0, 32),)),
        "short_filter": gaussian(splits[1], (SHORT, 3 * C), SHORT ** -0.5, 3.5),
        "long_filter": draw_long_filter(jax.random.fold_in(splits[4], 71), 0),
        "skip": jnp.clip(1.0 + 0.18 * jax.random.normal(splits[3], (C,), jnp.float32), 0.1, 1.9),
    }


TWO_PI = 2.0 * math.pi


def turn_table(rows, cols, length):
    product = (rows * cols) % length
    angle = product.astype(jnp.float32) * (TWO_PI / length)
    return jnp.cos(angle), jnp.sin(angle)


def counting(count):
    return jnp.arange(count, dtype=jnp.int32)


def rounded(table):
    narrow = lax.optimization_barrier(table.astype(jnp.bfloat16))
    return narrow.astype(jnp.float32)


def widened(values):
    return values.astype(jnp.float32)


def reference(projected, short_filter, long_filter, skip):
    segments = N_OUTER * N_INNER
    tap_count = short_filter.shape[0]
    width_block = math.gcd(C, 128)
    block_count = C // width_block
    cos_first, sin_first = turn_table(counting(BLOCKS)[:, None], counting(segments)[None, :], BLOCKS)
    cos_first, sin_first = rounded(cos_first), rounded(sin_first)
    cos_local, sin_local = turn_table(counting(TOK_DEV)[:, None], counting(TOK_DEV)[None, :], TOK_DEV)
    cos_local, sin_local = rounded(cos_local), rounded(sin_local)
    cos_last, sin_last = turn_table(counting(segments)[:, None], counting(BLOCKS)[None, :], BLOCKS)
    cos_last, sin_last = rounded(cos_last), rounded(sin_last)
    turn_cos, turn_sin = turn_table(counting(BLOCKS)[:, None], counting(TOK_DEV)[None, :], TRANSFORM)
    turn_cos = turn_cos[:, :, None]
    turn_sin = turn_sin[:, :, None]

    def featurize(columns, weights):
        padded = jnp.concatenate([jnp.zeros((tap_count - 1, width_block), jnp.bfloat16), columns], 0)
        summed = jnp.zeros((SEQ, width_block), jnp.float32)
        for tap_index in range(tap_count):
            offset = tap_count - 1 - tap_index
            summed = summed + weights[tap_index].astype(jnp.float32) * padded[offset:offset + SEQ].astype(jnp.float32)
        return summed

    def first_section(values):
        stacked = widened(values.reshape(segments, TOK_DEV, width_block))
        real_part = jnp.einsum('kb,bac->kac', cos_first, stacked)
        imag_part = -jnp.einsum('kb,bac->kac', sin_first, stacked)
        out_real = (real_part * turn_cos + imag_part * turn_sin).astype(jnp.bfloat16)
        out_imag = (imag_part * turn_cos - real_part * turn_sin).astype(jnp.bfloat16)
        return out_real, out_imag

    def local_section(real_half, imag_half):
        real_part = widened(real_half)
        imag_part = widened(imag_half)
        spec_real = jnp.einsum('ua,kac->kuc', cos_local, real_part) + jnp.einsum('ua,kac->kuc', sin_local, imag_part)
        spec_imag = jnp.einsum('ua,kac->kuc', cos_local, imag_part) - jnp.einsum('ua,kac->kuc', sin_local, real_part)
        return spec_real, spec_imag

    def one_block(block_index):
        offset = block_index * width_block
        query_cols = lax.dynamic_slice_in_dim(projected, offset, width_block, 1)
        key_cols = lax.dynamic_slice_in_dim(projected, offset + C, width_block, 1)
        value_cols = lax.dynamic_slice_in_dim(projected, offset + 2 * C, width_block, 1)
        query_taps = lax.dynamic_slice_in_dim(short_filter, offset, width_block, 1)
        key_taps = lax.dynamic_slice_in_dim(short_filter, offset + C, width_block, 1)
        value_taps = lax.dynamic_slice_in_dim(short_filter, offset + 2 * C, width_block, 1)
        query_rows = featurize(query_cols, query_taps)
        gated_rows = (featurize(key_cols, key_taps) * featurize(value_cols, value_taps)).astype(jnp.bfloat16)
        filter_cols = lax.dynamic_slice_in_dim(long_filter, offset, width_block, 1)
        signal_real, signal_imag = local_section(*first_section(gated_rows))
        filter_real, filter_imag = local_section(*first_section(filter_cols))
        product_real = widened((signal_real * filter_real - signal_imag * filter_imag).astype(jnp.bfloat16))
        product_imag = widened((signal_real * filter_imag + signal_imag * filter_real).astype(jnp.bfloat16))
        back_real = jnp.einsum('au,kuc->kac', cos_local, product_real) - jnp.einsum('au,kuc->kac', sin_local, product_imag)
        back_imag = jnp.einsum('au,kuc->kac', cos_local, product_imag) + jnp.einsum('au,kuc->kac', sin_local, product_real)
        first_real = widened((back_real * turn_cos - back_imag * turn_sin).astype(jnp.bfloat16))
        first_imag = widened((back_imag * turn_cos + back_real * turn_sin).astype(jnp.bfloat16))
        long_conv = (jnp.einsum('bk,kac->bac', cos_last, first_real) - jnp.einsum('bk,kac->bac', sin_last, first_imag)) * (1.0 / TRANSFORM)
        long_conv = long_conv.astype(jnp.bfloat16).reshape(SEQ, width_block)
        skip_gain = lax.dynamic_slice_in_dim(skip, offset, width_block, 0)
        mixed_cols = query_rows * (long_conv.astype(jnp.float32) + skip_gain[None, :] * gated_rows.astype(jnp.float32))
        return mixed_cols.astype(jnp.bfloat16)

    outputs = lax.map(one_block, counting(block_count))
    return jnp.transpose(outputs, (1, 0, 2)).reshape(SEQ, C)
```

```python
import functools
import math

import jax
import jax.numpy as jnp
import numpy as np
from jax import lax
from jax.experimental import pallas as pl
from jax.experimental.pallas import tpu as pltpu
from jax.sharding import PartitionSpec as P

TWO_PI = 2.0 * math.pi
MESH = pl.DeviceIdType.MESH
LANES = 128
ROWS = 16
RADIX = 8


class Cx:
    def __init__(self, re, im=None):
        self.re, self.im = re, im

    def __add__(self, other):
        if self.im is None:
            im = other.im
        elif other.im is None:
            im = self.im
        else:
            im = self.im + other.im
        return Cx(self.re + other.re, im)

    def __sub__(self, other):
        if other.im is None:
            im = self.im
        elif self.im is None:
            im = -other.im
        else:
            im = self.im - other.im
        return Cx(self.re - other.re, im)

    def conj(self):
        return Cx(self.re, None if self.im is None else -self.im)

    def times(self, turns, length):
        turns = turns % length
        if turns == 0:
            return self
        if 2 * turns == length:
            return Cx(-self.re, None if self.im is None else -self.im)
        cos, sin = math.cos(TWO_PI * turns / length), math.sin(TWO_PI * turns / length)
        if self.im is None:
            return Cx(self.re * cos, self.re * sin)
        if 8 * turns % length == 0 and 4 * turns % length != 0:
            half = math.sqrt(0.5)
            one, two = self.re * half, self.im * half
            signs = (round(cos / half), round(sin / half))
            re = {(1, 1): one - two, (1, -1): one + two, (-1, 1): -(one + two), (-1, -1): two - one}
            im = {(1, 1): one + two, (1, -1): two - one, (-1, 1): one - two, (-1, -1): -(one + two)}
            return Cx(re[signs], im[signs])
        return Cx(self.re * cos - self.im * sin, self.re * sin + self.im * cos)

    def plus_i(self, other, sign):
        if other.im is None:
            re = self.re
        else:
            re = self.re - other.im if sign > 0 else self.re + other.im
        turned = other.re if sign > 0 else -other.re
        return Cx(re, turned if self.im is None else self.im + turned)


def dft4(z, sign):
    s, t, u, v = z[0] + z[2], z[0] - z[2], z[1] + z[3], z[1] - z[3]
    return [s + u, t.plus_i(v, sign), s - u, t.plus_i(v, -sign)]


def dft8(z, sign):
    even, odd = dft4(z[0::2], sign), dft4(z[1::2], sign)
    out = [None] * 8
    for k in range(4):
        if k == 2:
            out[2], out[6] = even[2].plus_i(odd[2], sign), even[2].plus_i(odd[2], -sign)
        else:
            turned = odd[k].times(sign * k, 8)
            out[k], out[k + 4] = even[k] + turned, even[k] - turned
    return out


def forward64(x):
    half = math.sqrt(0.5)
    first = [[None] * 8 for _ in range(5)]
    for b in range(8):
        x0, x1, x2, x3 = x[b], x[b + 8], x[b + 16], x[b + 24]
        p, q, d = x0 + x2, x1 + x3, x1 - x3
        e, f = q * half, d * half
        first[0][b] = Cx(p + q)
        first[4][b] = Cx(p - q)
        first[2][b] = Cx(x0 - x2, -d)
        first[1][b] = Cx(x0 + f, -(e + x2))
        first[3][b] = Cx(x0 - f, x2 - e)
    out = {}
    for k1 in range(5):
        done = dft8([first[k1][b].times(-b * k1, 64) for b in range(8)], -1)
        for k0 in range(8):
            freq = k1 + 8 * k0
            if freq <= 32:
                out[freq] = done[k0]
            elif k1 not in (0, 4):
                out[64 - freq] = done[k0].conj()
    return out


def backward64(spec):
    half = math.sqrt(0.5)
    held = [None] * 5
    for k1 in range(5):
        values = []
        for k0 in range(8):
            freq = k1 + 8 * k0
            values.append(spec[freq] if freq <= 32 else spec[64 - freq].conj())
        done = dft8(values, 1)
        held[k1] = [done[b].times(b * k1, 64) for b in range(8)]
    out = [None] * 32
    for b in range(8):
        h0, h4 = held[0][b].re, held[4][b].re
        h1, h2, h3 = held[1][b], held[2][b], held[3][b]
        plus, minus = h0 + h4, h0 - h4
        a1, a3 = (h1.re - h3.re), (h1.im + h3.im)
        out[b] = plus + 2.0 * (h1.re + h2.re + h3.re)
        out[b + 16] = plus + 2.0 * (h3.im - h1.im - h2.re)
        out[b + 8] = minus + 2.0 * (half * (a1 - a3) - h2.im)
        out[b + 24] = minus + 2.0 * (h2.im - half * (a1 + a3))
    return out


def kernel(
    n, n_inner, proj_hbm, filt_hbm, taps_ref, skip_ref, fwd_ref, bwd_ref, turn_ref, out_ref,
    proj, halo, filt_in, gate_in, gate_out, conv_out, conv_in, first, fspec, back, turn, query,
    proj_sem, own_sem, halo_send, halo_recv, f_send, f_recv, g_send, g_recv, y_send, y_recv,
):
    tok = proj.shape[0]
    width = filt_hbm.shape[1]
    freqs = first.shape[0]
    outer, inner = lax.axis_index("outer"), lax.axis_index("inner")
    me = outer * n_inner + inner

    def place(device):
        return (device // n_inner, device % n_inner)

    def partner(step):
        return lax.rem(me + step, n)

    def columns(block, part=0):
        return pl.ds(pl.multiple_of(part * width + block * LANES, LANES), LANES)

    def each_partner(body):
        def run(step, carry):
            body(partner(step))
            return carry
        lax.fori_loop(1, n, run, 0)

    def halo_copy(to):
        return pltpu.make_async_remote_copy(
            src_ref=proj_hbm.at[pl.ds(tok - ROWS, ROWS), :], dst_ref=halo,
            send_sem=halo_send, recv_sem=halo_recv, device_id=place(to), device_id_type=MESH,
        )

    def filter_copy(to, slot, sem):
        return pltpu.make_async_remote_copy(
            src_ref=filt_hbm.at[:, columns(to)], dst_ref=filt_in.at[slot],
            send_sem=f_send.at[to], recv_sem=f_recv.at[sem], device_id=place(to), device_id_type=MESH,
        )

    def gate_copy(to, slot, sem):
        return pltpu.make_async_remote_copy(
            src_ref=gate_out.at[to], dst_ref=gate_in.at[slot],
            send_sem=g_send.at[to], recv_sem=g_recv.at[sem], device_id=place(to), device_id_type=MESH,
        )

    def conv_copy(to, slot, sem):
        return pltpu.make_async_remote_copy(
            src_ref=conv_out.at[to], dst_ref=conv_in.at[slot],
            send_sem=y_send.at[to], recv_sem=y_recv.at[sem], device_id=place(to), device_id_type=MESH,
        )

    load = pltpu.make_async_copy(proj_hbm, proj, proj_sem)
    load.start()
    own = pltpu.make_async_copy(filt_hbm.at[:, columns(me)], filt_in.at[me], own_sem)
    own.start()

    barrier = pltpu.get_barrier_semaphore()
    each_partner(lambda to: pl.semaphore_signal(
        barrier, inc=1, device_id=place(to), device_id_type=MESH))
    pl.semaphore_wait(barrier, n - 1)

    @pl.when(me < n - 1)
    def _():
        halo_copy(me + 1).start()

    each_partner(lambda to: filter_copy(to, me, me).start())

    load.wait()

    @pl.when(me == 0)
    def _():
        halo[...] = jnp.zeros_like(halo)

    @pl.when(me > 0)
    def _():
        halo_copy(me).wait_recv()

    def featured(block, part):
        cols = columns(block, part)
        taps = taps_ref[:, cols].astype(jnp.float32)
        rows = jnp.concatenate(
            [halo[:, cols].astype(jnp.float32), proj[:, cols].astype(jnp.float32)], 0)
        count = taps.shape[0]
        total = None
        for tap in range(count):
            start = ROWS - tap
            term = taps[tap:tap + 1] * rows[start:start + tok]
            total = term if total is None else total + term
        return total

    def gate(block):
        return (featured(block, 1) * featured(block, 2)).astype(jnp.bfloat16)

    def send_gate(to):
        gate_out[to] = gate(to)
        gate_copy(to, me, me).start()

    each_partner(send_gate)
    own_gate = gate(me)
    gate_out[me] = own_gate
    gate_in[me] = own_gate

    for freq in range(freqs):
        for part in range(2):
            turn[freq, part] = jnp.broadcast_to(
                turn_ref[part][:, freq:freq + 1], (tok, LANES))

    def ask(block, carry):
        query[block] = featured(block, 0)
        return carry

    lax.fori_loop(0, n, ask, 0)

    def first_section(source):
        def run(tile, carry):
            rows = pl.ds(pl.multiple_of(tile * ROWS, ROWS), ROWS)
            low = pl.ds(pl.multiple_of(tok + tile * ROWS, ROWS), ROWS)
            spec = forward64([source[b, rows, :].astype(jnp.float32) for b in range(n)])
            for freq in range(freqs):
                cos, sin = turn[freq, 0, rows, :], turn[freq, 1, rows, :]
                z = spec[freq]
                if z.im is None:
                    re, im = z.re * cos, -(z.re * sin)
                else:
                    re, im = z.re * cos + z.im * sin, z.im * cos - z.re * sin
                first[freq, rows, :] = re.astype(jnp.bfloat16)
                first[freq, low, :] = im.astype(jnp.bfloat16)
            return carry
        lax.fori_loop(0, tok // ROWS, run, 0)

    own.wait()
    each_partner(lambda src: filter_copy(src, src, src).wait_recv())
    first_section(filt_in)

    def filter_spectrum(freq, carry):
        fspec[freq] = jnp.dot(fwd_ref[...], first[freq], preferred_element_type=jnp.float32)
        return carry

    lax.fori_loop(0, freqs, filter_spectrum, 0)

    each_partner(lambda src: gate_copy(src, src, src).wait_recv())
    first_section(gate_in)

    def through(freq, carry):
        spec = jnp.dot(fwd_ref[...], first[freq], preferred_element_type=jnp.float32)
        sr, si = spec[:tok], spec[tok:]
        fr, fi = fspec[freq, :tok], fspec[freq, tok:]
        product = jnp.concatenate([sr * fr - si * fi, sr * fi + si * fr], 0).astype(jnp.bfloat16)
        result = jnp.dot(bwd_ref[...], product, preferred_element_type=jnp.float32)
        br, bi = result[:tok], result[tok:]
        cos, sin = turn[freq, 0], turn[freq, 1]
        back[freq, :tok] = br * cos - bi * sin
        back[freq, tok:] = bi * cos + br * sin
        return carry

    lax.fori_loop(0, freqs, through, 0)

    scale = 1.0 / (2 * n * tok)

    def last_section(tile, carry):
        rows = pl.ds(pl.multiple_of(tile * ROWS, ROWS), ROWS)
        low = pl.ds(pl.multiple_of(tok + tile * ROWS, ROWS), ROWS)
        done = backward64([Cx(back[freq, rows, :], back[freq, low, :]) for freq in range(freqs)])
        for b in range(n):
            conv_out[b, rows, :] = (done[b] * scale).astype(jnp.bfloat16)
        return carry

    lax.fori_loop(0, tok // ROWS, last_section, 0)

    each_partner(lambda to: conv_copy(to, me, me).start())

    def finish(block, rows):
        cols = columns(block)
        mixed = query[block] * (
            rows.astype(jnp.float32) + skip_ref[:, cols] * gate_out[block].astype(jnp.float32))
        out_ref[:, cols] = mixed.astype(jnp.bfloat16)

    finish(me, conv_out[me])

    def take(src):
        conv_copy(src, src, src).wait_recv()
        finish(src, conv_in[src])

    each_partner(take)

    @pl.when(me < n - 1)
    def _():
        halo_copy(me + 1).wait_send()

    def sent(to):
        filter_copy(to, me, me).wait_send()
        gate_copy(to, me, me).wait_send()
        conv_copy(to, me, me).wait_send()

    each_partner(sent)


def cosines(rows, cols, length):
    angle = (np.arange(rows)[:, None] * np.arange(cols)[None, :] % length) * (TWO_PI / length)
    return np.cos(angle), np.sin(angle)


def by_channels(projected, short_filter, long_filter, skip):
    n_inner = lax.axis_size("inner")
    n = lax.axis_size("outer") * n_inner
    tok, width = long_filter.shape
    freqs = n + 1
    cos, sin = cosines(tok, tok, tok)
    forward = np.block([[cos, sin], [-sin, cos]]).astype(jnp.bfloat16)
    backward = np.block([[cos, -sin], [sin, cos]]).astype(jnp.bfloat16)
    turns = np.stack(cosines(tok, LANES, 2 * n * tok)).astype(np.float32)
    vmem = pl.BlockSpec(memory_space=pltpu.VMEM)
    hbm = pl.BlockSpec(memory_space=pl.ANY)
    block = (n, tok, LANES)
    dma = pltpu.SemaphoreType.DMA
    return pl.pallas_call(
        functools.partial(kernel, n, n_inner),
        out_shape=jax.ShapeDtypeStruct((tok, width), jnp.bfloat16),
        in_specs=[hbm, hbm] + [vmem] * 5,
        out_specs=vmem,
        scratch_shapes=[
            pltpu.VMEM(projected.shape, jnp.bfloat16),
            pltpu.VMEM((ROWS, projected.shape[1]), jnp.bfloat16),
            pltpu.VMEM(block, jnp.bfloat16),
            pltpu.VMEM(block, jnp.bfloat16),
            pltpu.VMEM(block, jnp.bfloat16),
            pltpu.VMEM(block, jnp.bfloat16),
            pltpu.VMEM(block, jnp.bfloat16),
            pltpu.VMEM((freqs, 2 * tok, LANES), jnp.bfloat16),
            pltpu.VMEM((freqs, 2 * tok, LANES), jnp.float32),
            pltpu.VMEM((freqs, 2 * tok, LANES), jnp.float32),
            pltpu.VMEM((freqs, 2, tok, LANES), jnp.float32),
            pltpu.VMEM(block, jnp.float32),
            dma, dma, dma, dma,
            dma((n,)), dma((n,)), dma((n,)), dma((n,)), dma((n,)), dma((n,)),
        ],
        compiler_params=pltpu.CompilerParams(
            collective_id=0, has_side_effects=True, vmem_limit_bytes=56 * 1024 * 1024),
        cost_estimate=pl.CostEstimate(
            flops=2 * 3 * freqs * (2 * tok) ** 2 * LANES,
            bytes_accessed=10 * tok * width, transcendentals=0),
    )(projected, long_filter, short_filter, skip[None, :],
      jnp.asarray(forward), jnp.asarray(backward), jnp.asarray(turns))


def passed_along(value, axis, by):
    length = lax.axis_size(axis)
    pairs = [(i, i + by) for i in range(length) if 0 <= i + by < length]
    return lax.ppermute(value, axis, pairs)


def turn_table(rows, cols, length):
    product = rows * cols % length
    angle = product.astype(jnp.float32) * (TWO_PI / length)
    return (jnp.cos(angle), jnp.sin(angle))


def counting(count):
    return jnp.arange(count, dtype=jnp.int32)


def narrowed(table_pair):
    return (table_pair[0].astype(jnp.bfloat16), table_pair[1].astype(jnp.bfloat16))


def contract(form, table, values):
    return jnp.einsum(form, table, values, preferred_element_type=jnp.float32)


def shards(projected, short_filter, long_filter, skip):
    outer_count = lax.axis_size("outer")
    inner_count = lax.axis_size("inner")
    segments = outer_count * inner_count
    tok_rows, width_cols = long_filter.shape
    local_rows = tok_rows // segments
    freq_rows = 2 * segments
    freq_local = 2
    transform = freq_rows * tok_rows
    position = lax.axis_index(("outer", "inner"))
    tap_count = short_filter.shape[0]
    rim_count = tap_count - 1
    previous_rows = passed_along(projected[tok_rows - rim_count :], ("outer", "inner"), 1)
    extended = jnp.concatenate([previous_rows, projected], 0)
    featured = jnp.zeros(projected.shape, jnp.float32)
    for tap_index in range(tap_count):
        offset = rim_count - tap_index
        featured = featured + short_filter[tap_index].astype(jnp.float32) * extended[
            offset : offset + tok_rows
        ].astype(jnp.float32)
    query_rows = featured[:, :width_cols]
    gated_rows = (featured[:, width_cols : 2 * width_cols] * featured[:, 2 * width_cols :]).astype(
        jnp.bfloat16
    )
    cos_first, sin_first = narrowed(
        turn_table(counting(freq_rows)[:, None], counting(segments)[None, :], freq_rows)
    )
    owned_rows = position * local_rows + counting(local_rows)
    turn_cos, turn_sin = turn_table(counting(freq_rows)[:, None], owned_rows[None, :], transform)
    turn_cos = turn_cos[:, :, None]
    turn_sin = turn_sin[:, :, None]
    cos_local, sin_local = narrowed(
        turn_table(counting(tok_rows)[:, None], counting(tok_rows)[None, :], tok_rows)
    )
    owned_freqs = position * freq_local + counting(freq_local)
    back_cos, back_sin = turn_table(owned_freqs[:, None], counting(tok_rows)[None, :], transform)
    back_cos = back_cos[:, :, None]
    back_sin = back_sin[:, :, None]
    cos_last, sin_last = narrowed(
        turn_table(counting(segments)[:, None], counting(freq_rows)[None, :], freq_rows)
    )

    def first_section(stacked):
        real_part = contract("kb,bac->kac", cos_first, stacked)
        imag_part = -contract("kb,bac->kac", sin_first, stacked)
        out_real = (real_part * turn_cos + imag_part * turn_sin).astype(jnp.bfloat16)
        out_imag = (imag_part * turn_cos - real_part * turn_sin).astype(jnp.bfloat16)
        return (out_real, out_imag)

    def forward_local(real_half, imag_half):
        spec_real = contract("ua,kac->kuc", cos_local, real_half) + contract(
            "ua,kac->kuc", sin_local, imag_half
        )
        spec_imag = contract("ua,kac->kuc", cos_local, imag_half) - contract(
            "ua,kac->kuc", sin_local, real_half
        )
        return (spec_real, spec_imag)

    moved = (
        lax.all_to_all(
            gated_rows.reshape(segments, local_rows, width_cols),
            ("outer", "inner"),
            split_axis=0,
            concat_axis=0,
            tiled=True,
        ),
        lax.all_to_all(
            long_filter.reshape(segments, local_rows, width_cols),
            ("outer", "inner"),
            split_axis=0,
            concat_axis=0,
            tiled=True,
        ),
    )
    signal_cols = moved[0]
    filter_cols = moved[1]
    signal_real, signal_imag = first_section(signal_cols)
    filter_real, filter_imag = first_section(filter_cols)
    spectral_pieces = (
        lax.all_to_all(signal_real, ("outer", "inner"), split_axis=0, concat_axis=1, tiled=True),
        lax.all_to_all(signal_imag, ("outer", "inner"), split_axis=0, concat_axis=1, tiled=True),
        lax.all_to_all(filter_real, ("outer", "inner"), split_axis=0, concat_axis=1, tiled=True),
        lax.all_to_all(filter_imag, ("outer", "inner"), split_axis=0, concat_axis=1, tiled=True),
    )
    signal_real, signal_imag = forward_local(spectral_pieces[0], spectral_pieces[1])
    filter_real, filter_imag = forward_local(spectral_pieces[2], spectral_pieces[3])
    product_real = (signal_real * filter_real - signal_imag * filter_imag).astype(jnp.bfloat16)
    product_imag = (signal_real * filter_imag + signal_imag * filter_real).astype(jnp.bfloat16)
    back_real = contract("au,kuc->kac", cos_local, product_real) - contract(
        "au,kuc->kac", sin_local, product_imag
    )
    back_imag = contract("au,kuc->kac", cos_local, product_imag) + contract(
        "au,kuc->kac", sin_local, product_real
    )
    out_real = (back_real * back_cos - back_imag * back_sin).astype(jnp.bfloat16)
    out_imag = (back_imag * back_cos + back_real * back_sin).astype(jnp.bfloat16)
    moved = (
        lax.all_to_all(out_real, ("outer", "inner"), split_axis=1, concat_axis=0, tiled=True),
        lax.all_to_all(out_imag, ("outer", "inner"), split_axis=1, concat_axis=0, tiled=True),
    )
    rows_real = moved[0]
    rows_imag = moved[1]
    long_conv = (
        contract("bk,kac->bac", cos_last, rows_real) - contract("bk,kac->bac", sin_last, rows_imag)
    ) * (1.0 / transform)
    moved = lax.all_to_all(
        long_conv.astype(jnp.bfloat16), ("outer", "inner"), split_axis=0, concat_axis=0, tiled=True
    )
    conv_rows = moved.reshape(tok_rows, width_cols)
    mixed = query_rows * (
        conv_rows.astype(jnp.float32) + skip[None, :] * gated_rows.astype(jnp.float32)
    )
    return mixed.astype(jnp.bfloat16)


def operator(projected, short_filter, long_filter, skip):
    segments = lax.axis_size("outer") * lax.axis_size("inner")
    tok_rows, width_cols = long_filter.shape
    if 2 * segments == RADIX * RADIX and tok_rows == LANES and width_cols == segments * LANES:
        return by_channels(projected, short_filter, long_filter, skip)
    return shards(projected, short_filter, long_filter, skip)


def solution(mesh):
    in_specs = (P(("outer", "inner"), None), P(), P(("outer", "inner"), None), P())
    out_specs = P(("outer", "inner"), None)
    return jax.shard_map(operator, mesh=mesh, in_specs=in_specs, out_specs=out_specs, check_vma=False)
```

```python
import functools
import math

import jax
import jax.numpy as jnp
import numpy as np
from jax import lax
from jax.experimental import pallas as pl
from jax.experimental.pallas import tpu as pltpu
from jax.sharding import PartitionSpec as P

TWO_PI = 2.0 * math.pi
MESH = pl.DeviceIdType.MESH
LANES = 128
HALF = LANES // 2
ROWS = 16
RADIX = 8


class Cx:
    def __init__(self, re, im=None):
        self.re, self.im = re, im

    def __add__(self, other):
        if self.im is None:
            im = other.im
        elif other.im is None:
            im = self.im
        else:
            im = self.im + other.im
        return Cx(self.re + other.re, im)

    def __sub__(self, other):
        if other.im is None:
            im = self.im
        elif self.im is None:
            im = -other.im
        else:
            im = self.im - other.im
        return Cx(self.re - other.re, im)

    def conj(self):
        return Cx(self.re, None if self.im is None else -self.im)

    def times(self, turns, length):
        turns = turns % length
        if turns == 0:
            return self
        if 2 * turns == length:
            return Cx(-self.re, None if self.im is None else -self.im)
        cos, sin = math.cos(TWO_PI * turns / length), math.sin(TWO_PI * turns / length)
        if self.im is None:
            return Cx(self.re * cos, self.re * sin)
        if 8 * turns % length == 0 and 4 * turns % length != 0:
            half = math.sqrt(0.5)
            one, two = self.re * half, self.im * half
            signs = (round(cos / half), round(sin / half))
            re = {(1, 1): one - two, (1, -1): one + two, (-1, 1): -(one + two), (-1, -1): two - one}
            im = {(1, 1): one + two, (1, -1): two - one, (-1, 1): one - two, (-1, -1): -(one + two)}
            return Cx(re[signs], im[signs])
        return Cx(self.re * cos - self.im * sin, self.re * sin + self.im * cos)

    def plus_i(self, other, sign):
        if other.im is None:
            re = self.re
        else:
            re = self.re - other.im if sign > 0 else self.re + other.im
        turned = other.re if sign > 0 else -other.re
        return Cx(re, turned if self.im is None else self.im + turned)


def dft4(z, sign):
    s, t, u, v = z[0] + z[2], z[0] - z[2], z[1] + z[3], z[1] - z[3]
    return [s + u, t.plus_i(v, sign), s - u, t.plus_i(v, -sign)]


def dft8(z, sign):
    even, odd = dft4(z[0::2], sign), dft4(z[1::2], sign)
    out = [None] * 8
    for k in range(4):
        if k == 2:
            out[2], out[6] = even[2].plus_i(odd[2], sign), even[2].plus_i(odd[2], -sign)
        else:
            turned = odd[k].times(sign * k, 8)
            out[k], out[k + 4] = even[k] + turned, even[k] - turned
    return out


def forward64(x):
    half = math.sqrt(0.5)
    first = [[None] * 8 for _ in range(5)]
    for b in range(8):
        x0, x1, x2, x3 = x[b], x[b + 8], x[b + 16], x[b + 24]
        p, q, d = x0 + x2, x1 + x3, x1 - x3
        e, f = q * half, d * half
        first[0][b] = Cx(p + q)
        first[4][b] = Cx(p - q)
        first[2][b] = Cx(x0 - x2, -d)
        first[1][b] = Cx(x0 + f, -(e + x2))
        first[3][b] = Cx(x0 - f, x2 - e)
    out = {}
    for k1 in range(5):
        done = dft8([first[k1][b].times(-b * k1, 64) for b in range(8)], -1)
        for k0 in range(8):
            freq = k1 + 8 * k0
            if freq <= 32:
                out[freq] = done[k0]
            elif k1 not in (0, 4):
                out[64 - freq] = done[k0].conj()
    return out


def backward64(spec):
    half = math.sqrt(0.5)
    held = [None] * 5
    for k1 in range(5):
        values = []
        for k0 in range(8):
            freq = k1 + 8 * k0
            values.append(spec[freq] if freq <= 32 else spec[64 - freq].conj())
        done = dft8(values, 1)
        held[k1] = [done[b].times(b * k1, 64) for b in range(8)]
    out = [None] * 32
    for b in range(8):
        h0, h4 = held[0][b].re, held[4][b].re
        h1, h2, h3 = held[1][b], held[2][b], held[3][b]
        plus, minus = h0 + h4, h0 - h4
        a1, a3 = (h1.re - h3.re), (h1.im + h3.im)
        out[b] = plus + 2.0 * (h1.re + h2.re + h3.re)
        out[b + 16] = plus + 2.0 * (h3.im - h1.im - h2.re)
        out[b + 8] = minus + 2.0 * (half * (a1 - a3) - h2.im)
        out[b + 24] = minus + 2.0 * (h2.im - half * (a1 + a3))
    return out


def swapped_halves(x, y):
    left = lax.broadcasted_iota(jnp.int32, x.shape, 1) < HALF
    return (
        jnp.where(left, x, pltpu.roll(y, HALF, 1)),
        jnp.where(left, pltpu.roll(x, HALF, 1), y),
    )


def kernel(
    n, n_inner, proj_hbm, filt_hbm, taps_ref, skip_ref, fwd_ref, bwd_ref, turn_ref, out_ref,
    proj, filt, halo, filt_out, gate_out, conv_out, filt_in, gate_in, conv_in,
    gated, first, fspec, back, turn, query,
    proj_sem, filt_sem, halo_send, halo_recv, f_send, f_recv, g_send, g_recv, y_send, y_recv,
):
    tok, width = filt.shape
    freqs = n + 1
    half_tok = tok // 2
    quads = first.shape[0]
    outer, inner = lax.axis_index("outer"), lax.axis_index("inner")
    me = outer * n_inner + inner

    def place(device):
        return (device // n_inner, device % n_inner)

    def columns(block, part=0):
        return pl.ds(pl.multiple_of(part * width + block * LANES, LANES), LANES)

    def each_partner(body):
        def run(step, carry):
            body(lax.rem(me + step, n))
            return carry
        lax.fori_loop(1, n, run, 0)

    def loop(count, body):
        def run(step, carry):
            body(step)
            return carry
        lax.fori_loop(0, count, run, 0)

    def halo_copy(to):
        return pltpu.make_async_remote_copy(
            src_ref=proj_hbm.at[pl.ds(tok - ROWS, ROWS), :], dst_ref=halo,
            send_sem=halo_send, recv_sem=halo_recv, device_id=place(to), device_id_type=MESH,
        )

    def chunk_copy(source, target, send, recv, half, to, slot):
        return pltpu.make_async_remote_copy(
            src_ref=source.at[half, to], dst_ref=target.at[half, slot],
            send_sem=send.at[half, to], recv_sem=recv.at[half, slot],
            device_id=place(to), device_id_type=MESH,
        )

    filter_copy = functools.partial(chunk_copy, filt_out, filt_in, f_send, f_recv)
    gate_copy = functools.partial(chunk_copy, gate_out, gate_in, g_send, g_recv)
    conv_copy = functools.partial(chunk_copy, conv_out, conv_in, y_send, y_recv)

    def send_all(copy, half):
        each_partner(lambda to: copy(half, to, me).start())

    def receive_all(copy, half):
        each_partner(lambda src: copy(half, src, src).wait_recv())

    load_filt = pltpu.make_async_copy(filt_hbm, filt, filt_sem)
    load_filt.start()
    load = pltpu.make_async_copy(proj_hbm, proj, proj_sem)
    load.start()

    barrier = pltpu.get_barrier_semaphore()
    each_partner(lambda to: pl.semaphore_signal(
        barrier, inc=1, device_id=place(to), device_id_type=MESH))
    load_filt.wait()
    pl.semaphore_wait(barrier, n - 1)

    @pl.when(me < n - 1)
    def _():
        halo_copy(me + 1).start()

    def packed(values):
        first_half, second_half = swapped_halves(values[:half_tok], values[half_tok:])
        return first_half.astype(jnp.bfloat16), second_half.astype(jnp.bfloat16)

    def pack_filter(block):
        return packed(filt[:, columns(block)].astype(jnp.float32))

    def send_filter(to):
        filt_out[0, to], filt_out[1, to] = pack_filter(to)
        filter_copy(0, to, me).start()

    each_partner(send_filter)
    filt_in[0, me], filt_in[1, me] = pack_filter(me)

    load.wait()

    @pl.when(me == 0)
    def _():
        halo[...] = jnp.zeros_like(halo)

    @pl.when(me > 0)
    def _():
        halo_copy(me).wait_recv()

    def featured(block, part):
        cols = columns(block, part)
        taps = taps_ref[:, cols].astype(jnp.float32)
        rows = jnp.concatenate(
            [halo[:, cols].astype(jnp.float32), proj[:, cols].astype(jnp.float32)], 0)
        total = None
        for tap in range(taps.shape[0]):
            start = ROWS - tap
            term = taps[tap:tap + 1] * rows[start:start + tok]
            total = term if total is None else total + term
        return total

    def make_gate(block):
        rounded = (featured(block, 1) * featured(block, 2)).astype(jnp.bfloat16)
        gated[block] = rounded
        return packed(rounded.astype(jnp.float32))

    def send_gate(to):
        gate_out[0, to], gate_out[1, to] = make_gate(to)
        gate_copy(0, to, me).start()

    each_partner(send_gate)
    gate_in[0, me], gate_in[1, me] = make_gate(me)

    left = lax.broadcasted_iota(jnp.int32, (half_tok, LANES), 1) < HALF
    for freq in range(freqs):
        for part in range(2):
            column = turn_ref[part][:, freq:freq + 1]
            turn[freq, part] = jnp.where(left, column[:half_tok], column[half_tok:])
    first[quads - 1] = jnp.zeros(first.shape[1:], first.dtype)

    def spot(tile, shift):
        return pl.ds(pl.multiple_of(shift + tile * ROWS, ROWS), ROWS)

    def pair_lanes(pair):
        return pair // 2, slice((pair % 2) * LANES, (pair % 2 + 1) * LANES)

    def first_section(source, half):
        def run(tile):
            rows = spot(tile, 0)
            spec = forward64([source[half, b, rows, :].astype(jnp.float32) for b in range(n)])

            def turned(freq):
                cos, sin = turn[freq, 0, rows, :], turn[freq, 1, rows, :]
                z = spec[freq]
                if z.im is None:
                    return z.re * cos, -(z.re * sin)
                return z.re * cos + z.im * sin, z.im * cos - z.re * sin

            for pair in range((freqs + 1) // 2):
                even = turned(2 * pair)
                odd = turned(2 * pair + 1) if 2 * pair + 1 < freqs else even
                quad, lanes = pair_lanes(pair)
                for part in range(2):
                    low, high = swapped_halves(even[part], odd[part])
                    first[quad, spot(tile, part * tok), lanes] = low.astype(jnp.bfloat16)
                    first[quad, spot(tile, part * tok + half_tok), lanes] = high.astype(jnp.bfloat16)
        loop(half_tok // ROWS, run)

    def spectrum(quad):
        return jnp.dot(fwd_ref[...], first[quad], preferred_element_type=jnp.float32)

    def filter_section(half):
        first_section(filt_in, half)
        for quad in range(quads):
            fspec[quad] = spectrum(quad)

    def signal_section(half):
        first_section(gate_in, half)
        for quad in range(quads):
            spec = spectrum(quad)
            sr, si = spec[:tok], spec[tok:]
            fr, fi = fspec[quad, :tok], fspec[quad, tok:]
            product = jnp.concatenate([sr * fr - si * fi, sr * fi + si * fr], 0).astype(jnp.bfloat16)
            back[quad] = jnp.dot(bwd_ref[...], product, preferred_element_type=jnp.float32)

    scale = 1.0 / (2 * n * tok)

    def last_section(half):
        def run(tile):
            rows = spot(tile, 0)
            spec = []
            for pair in range((freqs + 1) // 2):
                quad, lanes = pair_lanes(pair)
                parts = [
                    swapped_halves(
                        back[quad, spot(tile, part * tok), lanes],
                        back[quad, spot(tile, part * tok + half_tok), lanes])
                    for part in range(2)
                ]
                for odd in range(2):
                    freq = 2 * pair + odd
                    if freq < freqs:
                        re, im = parts[0][odd], parts[1][odd]
                        cos, sin = turn[freq, 0, rows, :], turn[freq, 1, rows, :]
                        spec.append(Cx(re * cos - im * sin, im * cos + re * sin))
            done = backward64(spec)
            for b in range(n):
                conv_out[half, b, rows, :] = (done[b] * scale).astype(jnp.bfloat16)
        loop(half_tok // ROWS, run)

    receive_all(filter_copy, 0)
    send_all(filter_copy, 1)
    filter_section(0)
    receive_all(gate_copy, 0)
    send_all(gate_copy, 1)
    signal_section(0)
    last_section(0)
    send_all(conv_copy, 0)

    def ask(block):
        query[block] = featured(block, 0)

    loop(n, ask)

    receive_all(filter_copy, 1)
    filter_section(1)
    receive_all(gate_copy, 1)
    signal_section(1)
    last_section(1)
    send_all(conv_copy, 1)

    def finish(block, source):
        cols = columns(block)
        rows = jnp.concatenate(swapped_halves(
            source[0, block].astype(jnp.float32), source[1, block].astype(jnp.float32)), 0)
        mixed = query[block] * (rows + skip_ref[:, cols] * gated[block].astype(jnp.float32))
        out_ref[:, cols] = mixed.astype(jnp.bfloat16)

    finish(me, conv_out)

    def take(src):
        conv_copy(0, src, src).wait_recv()
        conv_copy(1, src, src).wait_recv()
        finish(src, conv_in)

    each_partner(take)

    @pl.when(me < n - 1)
    def _():
        halo_copy(me + 1).wait_send()

    def sent(to):
        for half in range(2):
            filter_copy(half, to, me).wait_send()
            gate_copy(half, to, me).wait_send()
            conv_copy(half, to, me).wait_send()

    each_partner(sent)


def cosines(rows, cols, length):
    angle = (np.arange(rows)[:, None] * np.arange(cols)[None, :] % length) * (TWO_PI / length)
    return np.cos(angle), np.sin(angle)


def by_channels(projected, short_filter, long_filter, skip):
    n_inner = lax.axis_size("inner")
    n = lax.axis_size("outer") * n_inner
    tok, width = long_filter.shape
    freqs = n + 1
    cos, sin = cosines(tok, tok, tok)
    forward = np.block([[cos, sin], [-sin, cos]]).astype(jnp.bfloat16)
    backward = np.block([[cos, -sin], [sin, cos]]).astype(jnp.bfloat16)
    turns = np.stack(cosines(tok, LANES, 2 * n * tok)).astype(np.float32)
    vmem = pl.BlockSpec(memory_space=pltpu.VMEM)
    hbm = pl.BlockSpec(memory_space=pl.ANY)
    quads = -(-freqs // 4)
    chunks = pltpu.VMEM((2, n, tok // 2, LANES), jnp.bfloat16)
    dma = pltpu.SemaphoreType.DMA
    return pl.pallas_call(
        functools.partial(kernel, n, n_inner),
        out_shape=jax.ShapeDtypeStruct((tok, width), jnp.bfloat16),
        in_specs=[hbm, hbm] + [vmem] * 5,
        out_specs=vmem,
        scratch_shapes=[
            pltpu.VMEM(projected.shape, jnp.bfloat16),
            pltpu.VMEM(long_filter.shape, jnp.bfloat16),
            pltpu.VMEM((ROWS, projected.shape[1]), jnp.bfloat16),
            chunks, chunks, chunks, chunks, chunks, chunks,
            pltpu.VMEM((n, tok, LANES), jnp.bfloat16),
            pltpu.VMEM((quads, 2 * tok, 4 * HALF), jnp.bfloat16),
            pltpu.VMEM((quads, 2 * tok, 4 * HALF), jnp.float32),
            pltpu.VMEM((quads, 2 * tok, 4 * HALF), jnp.float32),
            pltpu.VMEM((freqs, 2, tok // 2, LANES), jnp.float32),
            pltpu.VMEM((n, tok, LANES), jnp.float32),
            dma, dma, dma, dma,
            dma((2, n)), dma((2, n)), dma((2, n)), dma((2, n)), dma((2, n)), dma((2, n)),
        ],
        compiler_params=pltpu.CompilerParams(
            collective_id=0, has_side_effects=True, vmem_limit_bytes=56 * 1024 * 1024),
        cost_estimate=pl.CostEstimate(
            flops=2 * 3 * freqs * (2 * tok) ** 2 * LANES,
            bytes_accessed=10 * tok * width, transcendentals=0),
    )(projected, long_filter, short_filter, skip[None, :],
      jnp.asarray(forward), jnp.asarray(backward), jnp.asarray(turns))


def passed_along(value, axis, by):
    length = lax.axis_size(axis)
    pairs = [(i, i + by) for i in range(length) if 0 <= i + by < length]
    return lax.ppermute(value, axis, pairs)


def turn_table(rows, cols, length):
    product = rows * cols % length
    angle = product.astype(jnp.float32) * (TWO_PI / length)
    return (jnp.cos(angle), jnp.sin(angle))


def counting(count):
    return jnp.arange(count, dtype=jnp.int32)


def narrowed(table_pair):
    return (table_pair[0].astype(jnp.bfloat16), table_pair[1].astype(jnp.bfloat16))


def contract(form, table, values):
    return jnp.einsum(form, table, values, preferred_element_type=jnp.float32)


def shards(projected, short_filter, long_filter, skip):
    outer_count = lax.axis_size("outer")
    inner_count = lax.axis_size("inner")
    segments = outer_count * inner_count
    tok_rows, width_cols = long_filter.shape
    local_rows = tok_rows // segments
    freq_rows = 2 * segments
    freq_local = 2
    transform = freq_rows * tok_rows
    position = lax.axis_index(("outer", "inner"))
    tap_count = short_filter.shape[0]
    rim_count = tap_count - 1
    previous_rows = passed_along(projected[tok_rows - rim_count :], ("outer", "inner"), 1)
    extended = jnp.concatenate([previous_rows, projected], 0)
    featured = jnp.zeros(projected.shape, jnp.float32)
    for tap_index in range(tap_count):
        offset = rim_count - tap_index
        featured = featured + short_filter[tap_index].astype(jnp.float32) * extended[
            offset : offset + tok_rows
        ].astype(jnp.float32)
    query_rows = featured[:, :width_cols]
    gated_rows = (featured[:, width_cols : 2 * width_cols] * featured[:, 2 * width_cols :]).astype(
        jnp.bfloat16
    )
    cos_first, sin_first = narrowed(
        turn_table(counting(freq_rows)[:, None], counting(segments)[None, :], freq_rows)
    )
    owned_rows = position * local_rows + counting(local_rows)
    turn_cos, turn_sin = turn_table(counting(freq_rows)[:, None], owned_rows[None, :], transform)
    turn_cos = turn_cos[:, :, None]
    turn_sin = turn_sin[:, :, None]
    cos_local, sin_local = narrowed(
        turn_table(counting(tok_rows)[:, None], counting(tok_rows)[None, :], tok_rows)
    )
    owned_freqs = position * freq_local + counting(freq_local)
    back_cos, back_sin = turn_table(owned_freqs[:, None], counting(tok_rows)[None, :], transform)
    back_cos = back_cos[:, :, None]
    back_sin = back_sin[:, :, None]
    cos_last, sin_last = narrowed(
        turn_table(counting(segments)[:, None], counting(freq_rows)[None, :], freq_rows)
    )

    def first_section(stacked):
        real_part = contract("kb,bac->kac", cos_first, stacked)
        imag_part = -contract("kb,bac->kac", sin_first, stacked)
        out_real = (real_part * turn_cos + imag_part * turn_sin).astype(jnp.bfloat16)
        out_imag = (imag_part * turn_cos - real_part * turn_sin).astype(jnp.bfloat16)
        return (out_real, out_imag)

    def forward_local(real_half, imag_half):
        spec_real = contract("ua,kac->kuc", cos_local, real_half) + contract(
            "ua,kac->kuc", sin_local, imag_half
        )
        spec_imag = contract("ua,kac->kuc", cos_local, imag_half) - contract(
            "ua,kac->kuc", sin_local, real_half
        )
        return (spec_real, spec_imag)

    moved = (
        lax.all_to_all(
            gated_rows.reshape(segments, local_rows, width_cols),
            ("outer", "inner"),
            split_axis=0,
            concat_axis=0,
            tiled=True,
        ),
        lax.all_to_all(
            long_filter.reshape(segments, local_rows, width_cols),
            ("outer", "inner"),
            split_axis=0,
            concat_axis=0,
            tiled=True,
        ),
    )
    signal_cols = moved[0]
    filter_cols = moved[1]
    signal_real, signal_imag = first_section(signal_cols)
    filter_real, filter_imag = first_section(filter_cols)
    spectral_pieces = (
        lax.all_to_all(signal_real, ("outer", "inner"), split_axis=0, concat_axis=1, tiled=True),
        lax.all_to_all(signal_imag, ("outer", "inner"), split_axis=0, concat_axis=1, tiled=True),
        lax.all_to_all(filter_real, ("outer", "inner"), split_axis=0, concat_axis=1, tiled=True),
        lax.all_to_all(filter_imag, ("outer", "inner"), split_axis=0, concat_axis=1, tiled=True),
    )
    signal_real, signal_imag = forward_local(spectral_pieces[0], spectral_pieces[1])
    filter_real, filter_imag = forward_local(spectral_pieces[2], spectral_pieces[3])
    product_real = (signal_real * filter_real - signal_imag * filter_imag).astype(jnp.bfloat16)
    product_imag = (signal_real * filter_imag + signal_imag * filter_real).astype(jnp.bfloat16)
    back_real = contract("au,kuc->kac", cos_local, product_real) - contract(
        "au,kuc->kac", sin_local, product_imag
    )
    back_imag = contract("au,kuc->kac", cos_local, product_imag) + contract(
        "au,kuc->kac", sin_local, product_real
    )
    out_real = (back_real * back_cos - back_imag * back_sin).astype(jnp.bfloat16)
    out_imag = (back_imag * back_cos + back_real * back_sin).astype(jnp.bfloat16)
    moved = (
        lax.all_to_all(out_real, ("outer", "inner"), split_axis=1, concat_axis=0, tiled=True),
        lax.all_to_all(out_imag, ("outer", "inner"), split_axis=1, concat_axis=0, tiled=True),
    )
    rows_real = moved[0]
    rows_imag = moved[1]
    long_conv = (
        contract("bk,kac->bac", cos_last, rows_real) - contract("bk,kac->bac", sin_last, rows_imag)
    ) * (1.0 / transform)
    moved = lax.all_to_all(
        long_conv.astype(jnp.bfloat16), ("outer", "inner"), split_axis=0, concat_axis=0, tiled=True
    )
    conv_rows = moved.reshape(tok_rows, width_cols)
    mixed = query_rows * (
        conv_rows.astype(jnp.float32) + skip[None, :] * gated_rows.astype(jnp.float32)
    )
    return mixed.astype(jnp.bfloat16)


def operator(projected, short_filter, long_filter, skip):
    segments = lax.axis_size("outer") * lax.axis_size("inner")
    tok_rows, width_cols = long_filter.shape
    if 2 * segments == RADIX * RADIX and tok_rows == LANES and width_cols == segments * LANES:
        return by_channels(projected, short_filter, long_filter, skip)
    return shards(projected, short_filter, long_filter, skip)


def solution(mesh):
    in_specs = (P(("outer", "inner"), None), P(), P(("outer", "inner"), None), P())
    out_specs = P(("outer", "inner"), None)
    return jax.shard_map(operator, mesh=mesh, in_specs=in_specs, out_specs=out_specs, check_vma=False)
```

```python
import functools
import math

import jax
import jax.numpy as jnp
import numpy as np
from jax import lax
from jax.experimental import pallas as pl
from jax.experimental.pallas import tpu as pltpu
from jax.sharding import PartitionSpec as P

TWO_PI = 2.0 * math.pi
MESH = pl.DeviceIdType.MESH
LANES = 128
HALF = LANES // 2
ROWS = 16
RADIX = 8


class Cx:
    def __init__(self, re, im=None):
        self.re, self.im = re, im

    def __add__(self, other):
        if self.im is None:
            im = other.im
        elif other.im is None:
            im = self.im
        else:
            im = self.im + other.im
        return Cx(self.re + other.re, im)

    def __sub__(self, other):
        if other.im is None:
            im = self.im
        elif self.im is None:
            im = -other.im
        else:
            im = self.im - other.im
        return Cx(self.re - other.re, im)

    def conj(self):
        return Cx(self.re, None if self.im is None else -self.im)

    def times(self, turns, length):
        turns = turns % length
        if turns == 0:
            return self
        if 2 * turns == length:
            return Cx(-self.re, None if self.im is None else -self.im)
        cos, sin = math.cos(TWO_PI * turns / length), math.sin(TWO_PI * turns / length)
        if self.im is None:
            return Cx(self.re * cos, self.re * sin)
        if 8 * turns % length == 0 and 4 * turns % length != 0:
            half = math.sqrt(0.5)
            one, two = self.re * half, self.im * half
            signs = (round(cos / half), round(sin / half))
            re = {(1, 1): one - two, (1, -1): one + two, (-1, 1): -(one + two), (-1, -1): two - one}
            im = {(1, 1): one + two, (1, -1): two - one, (-1, 1): one - two, (-1, -1): -(one + two)}
            return Cx(re[signs], im[signs])
        return Cx(self.re * cos - self.im * sin, self.re * sin + self.im * cos)

    def plus_i(self, other, sign):
        if other.im is None:
            re = self.re
        else:
            re = self.re - other.im if sign > 0 else self.re + other.im
        turned = other.re if sign > 0 else -other.re
        return Cx(re, turned if self.im is None else self.im + turned)


def dft4(z, sign):
    s, t, u, v = z[0] + z[2], z[0] - z[2], z[1] + z[3], z[1] - z[3]
    return [s + u, t.plus_i(v, sign), s - u, t.plus_i(v, -sign)]


def dft8(z, sign):
    even, odd = dft4(z[0::2], sign), dft4(z[1::2], sign)
    out = [None] * 8
    for k in range(4):
        if k == 2:
            out[2], out[6] = even[2].plus_i(odd[2], sign), even[2].plus_i(odd[2], -sign)
        else:
            turned = odd[k].times(sign * k, 8)
            out[k], out[k + 4] = even[k] + turned, even[k] - turned
    return out


def forward64(x):
    half = math.sqrt(0.5)
    first = [[None] * 8 for _ in range(5)]
    for b in range(8):
        x0, x1, x2, x3 = x[b], x[b + 8], x[b + 16], x[b + 24]
        p, q, d = x0 + x2, x1 + x3, x1 - x3
        e, f = q * half, d * half
        first[0][b] = Cx(p + q)
        first[4][b] = Cx(p - q)
        first[2][b] = Cx(x0 - x2, -d)
        first[1][b] = Cx(x0 + f, -(e + x2))
        first[3][b] = Cx(x0 - f, x2 - e)
    out = {}
    for k1 in range(5):
        done = dft8([first[k1][b].times(-b * k1, 64) for b in range(8)], -1)
        for k0 in range(8):
            freq = k1 + 8 * k0
            if freq <= 32:
                out[freq] = done[k0]
            elif k1 not in (0, 4):
                out[64 - freq] = done[k0].conj()
    return out


def backward64(spec):
    half = math.sqrt(0.5)
    held = [None] * 5
    for k1 in range(5):
        values = []
        for k0 in range(8):
            freq = k1 + 8 * k0
            values.append(spec[freq] if freq <= 32 else spec[64 - freq].conj())
        done = dft8(values, 1)
        held[k1] = [done[b].times(b * k1, 64) for b in range(8)]
    out = [None] * 32
    for b in range(8):
        h0, h4 = held[0][b].re, held[4][b].re
        h1, h2, h3 = held[1][b], held[2][b], held[3][b]
        plus, minus = h0 + h4, h0 - h4
        a1, a3 = (h1.re - h3.re), (h1.im + h3.im)
        out[b] = plus + 2.0 * (h1.re + h2.re + h3.re)
        out[b + 16] = plus + 2.0 * (h3.im - h1.im - h2.re)
        out[b + 8] = minus + 2.0 * (half * (a1 - a3) - h2.im)
        out[b + 24] = minus + 2.0 * (h2.im - half * (a1 + a3))
    return out


def swapped_halves(x, y):
    left = lax.broadcasted_iota(jnp.int32, x.shape, 1) < HALF
    return (
        jnp.where(left, x, pltpu.roll(y, HALF, 1)),
        jnp.where(left, pltpu.roll(x, HALF, 1), y),
    )


def kernel(
    n, n_inner, proj_hbm, filt_hbm, taps_ref, skip_ref, fwd_ref, bwd_ref, turn_ref, out_ref,
    proj, filt, halo, filt_out, gate_out, conv_out, filt_in, gate_in, conv_in,
    gated, first, fspec, back, turn, query,
    proj_sem, filt_sem, halo_send, halo_recv, f_send, f_recv, g_send, g_recv, y_send, y_recv,
):
    tok, width = filt.shape
    freqs = n + 1
    half_tok = tok // 2
    quads = first.shape[0]
    outer, inner = lax.axis_index("outer"), lax.axis_index("inner")
    me = outer * n_inner + inner

    def place(device):
        return (device // n_inner, device % n_inner)

    def columns(block, part=0):
        return pl.ds(pl.multiple_of(part * width + block * LANES, LANES), LANES)

    n_z, n_outer = n_inner // 2, n // n_inner
    n_x = n_outer // 2
    x, core, z, y = outer // 2, outer % 2, inner // 2, inner % 2

    def partner(step):
        turn_of = step // n_z
        to_z = (z + step + (n_z // 2) * core) % n_z
        to_x = (x + turn_of + y) % n_x
        to_y = (y + turn_of // n_x + core) % 2
        to_core = (core + turn_of // (2 * n_x)) % 2
        return (to_x * 2 + to_core) * n_inner + to_z * 2 + to_y

    def each_partner(body):
        def run(step, carry):
            to = partner(step)

            @pl.when(to != me)
            def _():
                body(to)
            return carry
        lax.fori_loop(0, n, run, 0)

    def loop(count, body):
        def run(step, carry):
            body(step)
            return carry
        lax.fori_loop(0, count, run, 0)

    def halo_copy(to):
        return pltpu.make_async_remote_copy(
            src_ref=proj_hbm.at[pl.ds(tok - ROWS, ROWS), :], dst_ref=halo,
            send_sem=halo_send, recv_sem=halo_recv, device_id=place(to), device_id_type=MESH,
        )

    def chunk_copy(source, target, send, recv, half, to, slot):
        return pltpu.make_async_remote_copy(
            src_ref=source.at[half, to], dst_ref=target.at[half, slot],
            send_sem=send.at[half, to], recv_sem=recv.at[half, slot],
            device_id=place(to), device_id_type=MESH,
        )

    filter_copy = functools.partial(chunk_copy, filt_out, filt_in, f_send, f_recv)
    gate_copy = functools.partial(chunk_copy, gate_out, gate_in, g_send, g_recv)
    conv_copy = functools.partial(chunk_copy, conv_out, conv_in, y_send, y_recv)

    def send_all(copy, half):
        each_partner(lambda to: copy(half, to, me).start())

    def receive_all(copy, half):
        each_partner(lambda src: copy(half, src, src).wait_recv())

    load_filt = pltpu.make_async_copy(filt_hbm, filt, filt_sem)
    load_filt.start()
    load = pltpu.make_async_copy(proj_hbm, proj, proj_sem)
    load.start()

    barrier = pltpu.get_barrier_semaphore()
    each_partner(lambda to: pl.semaphore_signal(
        barrier, inc=1, device_id=place(to), device_id_type=MESH))
    load_filt.wait()
    pl.semaphore_wait(barrier, n - 1)

    @pl.when(me < n - 1)
    def _():
        halo_copy(me + 1).start()

    def packed(values):
        first_half, second_half = swapped_halves(values[:half_tok], values[half_tok:])
        return first_half.astype(jnp.bfloat16), second_half.astype(jnp.bfloat16)

    def pack_filter(block):
        return packed(filt[:, columns(block)].astype(jnp.float32))

    def send_filter(to):
        filt_out[0, to], filt_out[1, to] = pack_filter(to)
        filter_copy(0, to, me).start()

    each_partner(send_filter)
    filt_in[0, me], filt_in[1, me] = pack_filter(me)

    load.wait()

    @pl.when(me == 0)
    def _():
        halo[...] = jnp.zeros_like(halo)

    @pl.when(me > 0)
    def _():
        halo_copy(me).wait_recv()

    def featured(block, part):
        cols = columns(block, part)
        taps = taps_ref[:, cols].astype(jnp.float32)
        rows = jnp.concatenate(
            [halo[:, cols].astype(jnp.float32), proj[:, cols].astype(jnp.float32)], 0)
        total = None
        for tap in range(taps.shape[0]):
            start = ROWS - tap
            term = taps[tap:tap + 1] * rows[start:start + tok]
            total = term if total is None else total + term
        return total

    def make_gate(block):
        rounded = (featured(block, 1) * featured(block, 2)).astype(jnp.bfloat16)
        gated[block] = rounded
        return packed(rounded.astype(jnp.float32))

    def send_gate(to):
        gate_out[0, to], gate_out[1, to] = make_gate(to)
        gate_copy(0, to, me).start()

    each_partner(send_gate)
    gate_in[0, me], gate_in[1, me] = make_gate(me)

    left = lax.broadcasted_iota(jnp.int32, (half_tok, LANES), 1) < HALF
    for freq in range(freqs):
        for part in range(2):
            column = turn_ref[part][:, freq:freq + 1]
            turn[freq, part] = jnp.where(left, column[:half_tok], column[half_tok:])
    first[quads - 1] = jnp.zeros(first.shape[1:], first.dtype)

    def spot(tile, shift):
        return pl.ds(pl.multiple_of(shift + tile * ROWS, ROWS), ROWS)

    def pair_lanes(pair):
        return pair // 2, slice((pair % 2) * LANES, (pair % 2 + 1) * LANES)

    def first_section(source, half):
        def run(tile):
            rows = spot(tile, 0)
            spec = forward64([source[half, b, rows, :].astype(jnp.float32) for b in range(n)])

            def turned(freq):
                cos, sin = turn[freq, 0, rows, :], turn[freq, 1, rows, :]
                z = spec[freq]
                if z.im is None:
                    return z.re * cos, -(z.re * sin)
                return z.re * cos + z.im * sin, z.im * cos - z.re * sin

            for pair in range((freqs + 1) // 2):
                even = turned(2 * pair)
                odd = turned(2 * pair + 1) if 2 * pair + 1 < freqs else even
                quad, lanes = pair_lanes(pair)
                for part in range(2):
                    low, high = swapped_halves(even[part], odd[part])
                    first[quad, spot(tile, part * tok), lanes] = low.astype(jnp.bfloat16)
                    first[quad, spot(tile, part * tok + half_tok), lanes] = high.astype(jnp.bfloat16)
        loop(half_tok // ROWS, run)

    def spectrum(quad):
        return jnp.dot(fwd_ref[...], first[quad], preferred_element_type=jnp.float32)

    def filter_section(half):
        first_section(filt_in, half)
        for quad in range(quads):
            fspec[quad] = spectrum(quad)

    def signal_section(half):
        first_section(gate_in, half)
        for quad in range(quads):
            spec = spectrum(quad)
            sr, si = spec[:tok], spec[tok:]
            fr, fi = fspec[quad, :tok], fspec[quad, tok:]
            product = jnp.concatenate([sr * fr - si * fi, sr * fi + si * fr], 0).astype(jnp.bfloat16)
            back[quad] = jnp.dot(bwd_ref[...], product, preferred_element_type=jnp.float32)

    scale = 1.0 / (2 * n * tok)

    def last_section(half):
        def run(tile):
            rows = spot(tile, 0)
            spec = []
            for pair in range((freqs + 1) // 2):
                quad, lanes = pair_lanes(pair)
                parts = [
                    swapped_halves(
                        back[quad, spot(tile, part * tok), lanes],
                        back[quad, spot(tile, part * tok + half_tok), lanes])
                    for part in range(2)
                ]
                for odd in range(2):
                    freq = 2 * pair + odd
                    if freq < freqs:
                        re, im = parts[0][odd], parts[1][odd]
                        cos, sin = turn[freq, 0, rows, :], turn[freq, 1, rows, :]
                        spec.append(Cx(re * cos - im * sin, im * cos + re * sin))
            done = backward64(spec)
            for b in range(n):
                conv_out[half, b, rows, :] = (done[b] * scale).astype(jnp.bfloat16)
        loop(half_tok // ROWS, run)

    receive_all(filter_copy, 0)
    send_all(filter_copy, 1)
    filter_section(0)
    receive_all(gate_copy, 0)
    send_all(gate_copy, 1)
    signal_section(0)
    last_section(0)
    send_all(conv_copy, 0)

    def ask(block):
        query[block] = featured(block, 0)

    loop(n, ask)

    receive_all(filter_copy, 1)
    filter_section(1)
    receive_all(gate_copy, 1)
    signal_section(1)
    last_section(1)
    send_all(conv_copy, 1)

    def finish(block, source):
        cols = columns(block)
        rows = jnp.concatenate(swapped_halves(
            source[0, block].astype(jnp.float32), source[1, block].astype(jnp.float32)), 0)
        mixed = query[block] * (rows + skip_ref[:, cols] * gated[block].astype(jnp.float32))
        out_ref[:, cols] = mixed.astype(jnp.bfloat16)

    finish(me, conv_out)

    def take(src):
        conv_copy(0, src, src).wait_recv()
        conv_copy(1, src, src).wait_recv()
        finish(src, conv_in)

    each_partner(take)

    @pl.when(me < n - 1)
    def _():
        halo_copy(me + 1).wait_send()

    def sent(to):
        for half in range(2):
            filter_copy(half, to, me).wait_send()
            gate_copy(half, to, me).wait_send()
            conv_copy(half, to, me).wait_send()

    each_partner(sent)


def cosines(rows, cols, length):
    angle = (np.arange(rows)[:, None] * np.arange(cols)[None, :] % length) * (TWO_PI / length)
    return np.cos(angle), np.sin(angle)


def by_channels(projected, short_filter, long_filter, skip):
    n_inner = lax.axis_size("inner")
    n = lax.axis_size("outer") * n_inner
    tok, width = long_filter.shape
    freqs = n + 1
    cos, sin = cosines(tok, tok, tok)
    forward = np.block([[cos, sin], [-sin, cos]]).astype(jnp.bfloat16)
    backward = np.block([[cos, -sin], [sin, cos]]).astype(jnp.bfloat16)
    turns = np.stack(cosines(tok, LANES, 2 * n * tok)).astype(np.float32)
    vmem = pl.BlockSpec(memory_space=pltpu.VMEM)
    hbm = pl.BlockSpec(memory_space=pl.ANY)
    quads = -(-freqs // 4)
    chunks = pltpu.VMEM((2, n, tok // 2, LANES), jnp.bfloat16)
    dma = pltpu.SemaphoreType.DMA
    return pl.pallas_call(
        functools.partial(kernel, n, n_inner),
        out_shape=jax.ShapeDtypeStruct((tok, width), jnp.bfloat16),
        in_specs=[hbm, hbm] + [vmem] * 5,
        out_specs=vmem,
        scratch_shapes=[
            pltpu.VMEM(projected.shape, jnp.bfloat16),
            pltpu.VMEM(long_filter.shape, jnp.bfloat16),
            pltpu.VMEM((ROWS, projected.shape[1]), jnp.bfloat16),
            chunks, chunks, chunks, chunks, chunks, chunks,
            pltpu.VMEM((n, tok, LANES), jnp.bfloat16),
            pltpu.VMEM((quads, 2 * tok, 4 * HALF), jnp.bfloat16),
            pltpu.VMEM((quads, 2 * tok, 4 * HALF), jnp.float32),
            pltpu.VMEM((quads, 2 * tok, 4 * HALF), jnp.float32),
            pltpu.VMEM((freqs, 2, tok // 2, LANES), jnp.float32),
            pltpu.VMEM((n, tok, LANES), jnp.float32),
            dma, dma, dma, dma,
            dma((2, n)), dma((2, n)), dma((2, n)), dma((2, n)), dma((2, n)), dma((2, n)),
        ],
        compiler_params=pltpu.CompilerParams(
            collective_id=0, has_side_effects=True, vmem_limit_bytes=56 * 1024 * 1024),
        cost_estimate=pl.CostEstimate(
            flops=2 * 3 * freqs * (2 * tok) ** 2 * LANES,
            bytes_accessed=10 * tok * width, transcendentals=0),
    )(projected, long_filter, short_filter, skip[None, :],
      jnp.asarray(forward), jnp.asarray(backward), jnp.asarray(turns))


def passed_along(value, axis, by):
    length = lax.axis_size(axis)
    pairs = [(i, i + by) for i in range(length) if 0 <= i + by < length]
    return lax.ppermute(value, axis, pairs)


def turn_table(rows, cols, length):
    product = rows * cols % length
    angle = product.astype(jnp.float32) * (TWO_PI / length)
    return (jnp.cos(angle), jnp.sin(angle))


def counting(count):
    return jnp.arange(count, dtype=jnp.int32)


def narrowed(table_pair):
    return (table_pair[0].astype(jnp.bfloat16), table_pair[1].astype(jnp.bfloat16))


def contract(form, table, values):
    return jnp.einsum(form, table, values, preferred_element_type=jnp.float32)


def shards(projected, short_filter, long_filter, skip):
    outer_count = lax.axis_size("outer")
    inner_count = lax.axis_size("inner")
    segments = outer_count * inner_count
    tok_rows, width_cols = long_filter.shape
    local_rows = tok_rows // segments
    freq_rows = 2 * segments
    freq_local = 2
    transform = freq_rows * tok_rows
    position = lax.axis_index(("outer", "inner"))
    tap_count = short_filter.shape[0]
    rim_count = tap_count - 1
    previous_rows = passed_along(projected[tok_rows - rim_count :], ("outer", "inner"), 1)
    extended = jnp.concatenate([previous_rows, projected], 0)
    featured = jnp.zeros(projected.shape, jnp.float32)
    for tap_index in range(tap_count):
        offset = rim_count - tap_index
        featured = featured + short_filter[tap_index].astype(jnp.float32) * extended[
            offset : offset + tok_rows
        ].astype(jnp.float32)
    query_rows = featured[:, :width_cols]
    gated_rows = (featured[:, width_cols : 2 * width_cols] * featured[:, 2 * width_cols :]).astype(
        jnp.bfloat16
    )
    cos_first, sin_first = narrowed(
        turn_table(counting(freq_rows)[:, None], counting(segments)[None, :], freq_rows)
    )
    owned_rows = position * local_rows + counting(local_rows)
    turn_cos, turn_sin = turn_table(counting(freq_rows)[:, None], owned_rows[None, :], transform)
    turn_cos = turn_cos[:, :, None]
    turn_sin = turn_sin[:, :, None]
    cos_local, sin_local = narrowed(
        turn_table(counting(tok_rows)[:, None], counting(tok_rows)[None, :], tok_rows)
    )
    owned_freqs = position * freq_local + counting(freq_local)
    back_cos, back_sin = turn_table(owned_freqs[:, None], counting(tok_rows)[None, :], transform)
    back_cos = back_cos[:, :, None]
    back_sin = back_sin[:, :, None]
    cos_last, sin_last = narrowed(
        turn_table(counting(segments)[:, None], counting(freq_rows)[None, :], freq_rows)
    )

    def first_section(stacked):
        real_part = contract("kb,bac->kac", cos_first, stacked)
        imag_part = -contract("kb,bac->kac", sin_first, stacked)
        out_real = (real_part * turn_cos + imag_part * turn_sin).astype(jnp.bfloat16)
        out_imag = (imag_part * turn_cos - real_part * turn_sin).astype(jnp.bfloat16)
        return (out_real, out_imag)

    def forward_local(real_half, imag_half):
        spec_real = contract("ua,kac->kuc", cos_local, real_half) + contract(
            "ua,kac->kuc", sin_local, imag_half
        )
        spec_imag = contract("ua,kac->kuc", cos_local, imag_half) - contract(
            "ua,kac->kuc", sin_local, real_half
        )
        return (spec_real, spec_imag)

    moved = (
        lax.all_to_all(
            gated_rows.reshape(segments, local_rows, width_cols),
            ("outer", "inner"),
            split_axis=0,
            concat_axis=0,
            tiled=True,
        ),
        lax.all_to_all(
            long_filter.reshape(segments, local_rows, width_cols),
            ("outer", "inner"),
            split_axis=0,
            concat_axis=0,
            tiled=True,
        ),
    )
    signal_cols = moved[0]
    filter_cols = moved[1]
    signal_real, signal_imag = first_section(signal_cols)
    filter_real, filter_imag = first_section(filter_cols)
    spectral_pieces = (
        lax.all_to_all(signal_real, ("outer", "inner"), split_axis=0, concat_axis=1, tiled=True),
        lax.all_to_all(signal_imag, ("outer", "inner"), split_axis=0, concat_axis=1, tiled=True),
        lax.all_to_all(filter_real, ("outer", "inner"), split_axis=0, concat_axis=1, tiled=True),
        lax.all_to_all(filter_imag, ("outer", "inner"), split_axis=0, concat_axis=1, tiled=True),
    )
    signal_real, signal_imag = forward_local(spectral_pieces[0], spectral_pieces[1])
    filter_real, filter_imag = forward_local(spectral_pieces[2], spectral_pieces[3])
    product_real = (signal_real * filter_real - signal_imag * filter_imag).astype(jnp.bfloat16)
    product_imag = (signal_real * filter_imag + signal_imag * filter_real).astype(jnp.bfloat16)
    back_real = contract("au,kuc->kac", cos_local, product_real) - contract(
        "au,kuc->kac", sin_local, product_imag
    )
    back_imag = contract("au,kuc->kac", cos_local, product_imag) + contract(
        "au,kuc->kac", sin_local, product_real
    )
    out_real = (back_real * back_cos - back_imag * back_sin).astype(jnp.bfloat16)
    out_imag = (back_imag * back_cos + back_real * back_sin).astype(jnp.bfloat16)
    moved = (
        lax.all_to_all(out_real, ("outer", "inner"), split_axis=1, concat_axis=0, tiled=True),
        lax.all_to_all(out_imag, ("outer", "inner"), split_axis=1, concat_axis=0, tiled=True),
    )
    rows_real = moved[0]
    rows_imag = moved[1]
    long_conv = (
        contract("bk,kac->bac", cos_last, rows_real) - contract("bk,kac->bac", sin_last, rows_imag)
    ) * (1.0 / transform)
    moved = lax.all_to_all(
        long_conv.astype(jnp.bfloat16), ("outer", "inner"), split_axis=0, concat_axis=0, tiled=True
    )
    conv_rows = moved.reshape(tok_rows, width_cols)
    mixed = query_rows * (
        conv_rows.astype(jnp.float32) + skip[None, :] * gated_rows.astype(jnp.float32)
    )
    return mixed.astype(jnp.bfloat16)


def operator(projected, short_filter, long_filter, skip):
    segments = lax.axis_size("outer") * lax.axis_size("inner")
    tok_rows, width_cols = long_filter.shape
    if 2 * segments == RADIX * RADIX and tok_rows == LANES and width_cols == segments * LANES:
        return by_channels(projected, short_filter, long_filter, skip)
    return shards(projected, short_filter, long_filter, skip)


def solution(mesh):
    in_specs = (P(("outer", "inner"), None), P(), P(("outer", "inner"), None), P())
    out_specs = P(("outer", "inner"), None)
    return jax.shard_map(operator, mesh=mesh, in_specs=in_specs, out_specs=out_specs, check_vma=False)
```

```python
import functools
import math

import jax
import jax.numpy as jnp
import numpy as np
from jax import lax
from jax.experimental import pallas as pl
from jax.experimental.pallas import tpu as pltpu
from jax.sharding import PartitionSpec as P

TWO_PI = 2.0 * math.pi
MESH = pl.DeviceIdType.MESH
LANES = 128
HALF = LANES // 2
ROWS = 16
SUB = 8
RADIX = 8


class Cx:
    def __init__(self, re, im=None):
        self.re, self.im = re, im

    def __add__(self, other):
        if self.im is None:
            im = other.im
        elif other.im is None:
            im = self.im
        else:
            im = self.im + other.im
        return Cx(self.re + other.re, im)

    def __sub__(self, other):
        if other.im is None:
            im = self.im
        elif self.im is None:
            im = -other.im
        else:
            im = self.im - other.im
        return Cx(self.re - other.re, im)

    def conj(self):
        return Cx(self.re, None if self.im is None else -self.im)

    def times(self, turns, length):
        turns = turns % length
        if turns == 0:
            return self
        if 2 * turns == length:
            return Cx(-self.re, None if self.im is None else -self.im)
        cos, sin = math.cos(TWO_PI * turns / length), math.sin(TWO_PI * turns / length)
        if self.im is None:
            return Cx(self.re * cos, self.re * sin)
        if 8 * turns % length == 0 and 4 * turns % length != 0:
            half = math.sqrt(0.5)
            one, two = self.re * half, self.im * half
            signs = (round(cos / half), round(sin / half))
            re = {(1, 1): one - two, (1, -1): one + two, (-1, 1): -(one + two), (-1, -1): two - one}
            im = {(1, 1): one + two, (1, -1): two - one, (-1, 1): one - two, (-1, -1): -(one + two)}
            return Cx(re[signs], im[signs])
        return Cx(self.re * cos - self.im * sin, self.re * sin + self.im * cos)

    def plus_i(self, other, sign):
        if other.im is None:
            re = self.re
        else:
            re = self.re - other.im if sign > 0 else self.re + other.im
        turned = other.re if sign > 0 else -other.re
        return Cx(re, turned if self.im is None else self.im + turned)


def dft4(z, sign):
    s, t, u, v = z[0] + z[2], z[0] - z[2], z[1] + z[3], z[1] - z[3]
    return [s + u, t.plus_i(v, sign), s - u, t.plus_i(v, -sign)]


def dft8(z, sign):
    even, odd = dft4(z[0::2], sign), dft4(z[1::2], sign)
    out = [None] * 8
    for k in range(4):
        if k == 2:
            out[2], out[6] = even[2].plus_i(odd[2], sign), even[2].plus_i(odd[2], -sign)
        else:
            turned = odd[k].times(sign * k, 8)
            out[k], out[k + 4] = even[k] + turned, even[k] - turned
    return out


def forward64(x):
    half = math.sqrt(0.5)
    first = [[None] * 8 for _ in range(5)]
    for b in range(8):
        x0, x1, x2, x3 = x[b], x[b + 8], x[b + 16], x[b + 24]
        p, q, d = x0 + x2, x1 + x3, x1 - x3
        e, f = q * half, d * half
        first[0][b] = Cx(p + q)
        first[4][b] = Cx(p - q)
        first[2][b] = Cx(x0 - x2, -d)
        first[1][b] = Cx(x0 + f, -(e + x2))
        first[3][b] = Cx(x0 - f, x2 - e)
    out = {}
    for k1 in range(5):
        done = dft8([first[k1][b].times(-b * k1, 64) for b in range(8)], -1)
        for k0 in range(8):
            freq = k1 + 8 * k0
            if freq <= 32:
                out[freq] = done[k0]
            elif k1 not in (0, 4):
                out[64 - freq] = done[k0].conj()
    return out


def backward64(spec):
    half = math.sqrt(0.5)
    held = [None] * 5
    for k1 in range(5):
        values = []
        for k0 in range(8):
            freq = k1 + 8 * k0
            values.append(spec[freq] if freq <= 32 else spec[64 - freq].conj())
        done = dft8(values, 1)
        held[k1] = [done[b].times(b * k1, 64) for b in range(8)]
    out = [None] * 32
    for b in range(8):
        h0, h4 = held[0][b].re, held[4][b].re
        h1, h2, h3 = held[1][b], held[2][b], held[3][b]
        plus, minus = h0 + h4, h0 - h4
        a1, a3 = (h1.re - h3.re), (h1.im + h3.im)
        out[b] = plus + 2.0 * (h1.re + h2.re + h3.re)
        out[b + 16] = plus + 2.0 * (h3.im - h1.im - h2.re)
        out[b + 8] = minus + 2.0 * (half * (a1 - a3) - h2.im)
        out[b + 24] = minus + 2.0 * (h2.im - half * (a1 + a3))
    return out


def swapped_halves(x, y):
    left = lax.broadcasted_iota(jnp.int32, x.shape, 1) < HALF
    return (
        jnp.where(left, x, pltpu.roll(y, HALF, 1)),
        jnp.where(left, pltpu.roll(x, HALF, 1), y),
    )


def kernel(
    n, n_inner, proj_hbm, filt_hbm, taps_ref, skip_ref, fwd_ref, bwd_ref, turn_ref, out_ref,
    proj, filt, halo, halo_out, halo_in, filt_out, gate_out, conv_out, filt_in, gate_in, conv_in,
    gated, first, fspec, back, turn, query,
    proj_sem, filt_sem, halo_send, halo_recv, f_sems, g_sems, y_sems,
):
    tok, width = filt.shape
    freqs = n + 1
    half_tok = tok // 2
    quads = first.shape[0]
    outer, inner = lax.axis_index("outer"), lax.axis_index("inner")
    me = outer * n_inner + inner

    def columns(block, part=0):
        return pl.ds(pl.multiple_of(part * width + block * LANES, LANES), LANES)

    n_z = n_inner // 2
    n_x = n // n_inner // 2
    x, core = lax.div(outer, 2), lax.rem(outer, 2)
    z, y = lax.div(inner, 2), lax.rem(inner, 2)

    def partner(step):
        turn_of = lax.div(step, n_z)
        to_z = lax.rem(z + step + (n_z // 2) * core, n_z)
        to_x = lax.rem(x + turn_of + y, n_x)
        to_y = lax.rem(y + lax.div(turn_of, n_x) + core, 2)
        to_core = lax.rem(core + lax.div(turn_of, 2 * n_x), 2)
        to = (to_x * 2 + to_core, to_z * 2 + to_y)
        return to, to[0] * n_inner + to[1]

    def each_partner(body):
        def run(step, carry):
            to, number = partner(step)

            @pl.when(number != me)
            def _():
                body(to, number)
            return carry
        lax.fori_loop(0, n, run, 0)

    def loop(count, body):
        def run(step, carry):
            body(step)
            return carry
        lax.fori_loop(0, count, run, 0)

    def halo_copy(to):
        return pltpu.make_async_remote_copy(
            src_ref=halo_out, dst_ref=halo_in, send_sem=halo_send, recv_sem=halo_recv,
            device_id=(lax.div(to, n_inner), lax.rem(to, n_inner)), device_id_type=MESH,
        )

    def send(source, target, sems, half, to, number):
        pltpu.make_async_remote_copy(
            src_ref=source.at[half, number], dst_ref=target.at[half, me],
            send_sem=sems.at[0, half], recv_sem=sems.at[1, half],
            device_id=to, device_id_type=MESH,
        ).start()

    def wait_all(buffer, sems, way, half):
        chunks = buffer.at[half, pl.ds(0, n - 1)]
        pltpu.make_async_copy(chunks, chunks, sems.at[way, half]).wait()

    send_filter = functools.partial(send, filt_out, filt_in, f_sems)
    send_gate = functools.partial(send, gate_out, gate_in, g_sems)
    send_conv = functools.partial(send, conv_out, conv_in, y_sems)

    load = pltpu.make_async_copy(proj_hbm, proj, proj_sem)
    load.start()
    load_filt = pltpu.make_async_copy(filt_hbm, filt, filt_sem)
    load_filt.start()

    barrier = pltpu.get_barrier_semaphore()
    each_partner(lambda to, number: pl.semaphore_signal(
        barrier, inc=1, device_id=to, device_id_type=MESH))

    load.wait()
    blocks = proj.shape[1] // LANES
    for block in range(blocks):
        tail = proj[tok - ROWS:, block * LANES:(block + 1) * LANES].astype(jnp.float32)
        halo[2 * block:2 * block + 2, :] = tail[ROWS - 2:]
    halo_out[...] = halo[...].astype(jnp.bfloat16)

    load_filt.wait()
    pl.semaphore_wait(barrier, n - 1)

    @pl.when(me < n - 1)
    def _():
        halo_copy(me + 1).start()

    def packed(values):
        first_half, second_half = swapped_halves(values[:half_tok], values[half_tok:])
        return first_half.astype(jnp.bfloat16), second_half.astype(jnp.bfloat16)

    def pack_filter(block):
        return packed(filt[:, columns(block)].astype(jnp.float32))

    def start_filter(to, number):
        filt_out[0, number], filt_out[1, number] = pack_filter(number)
        send_filter(0, to, number)

    each_partner(start_filter)
    filt_in[0, me], filt_in[1, me] = pack_filter(me)

    @pl.when(me == 0)
    def _():
        halo[...] = jnp.zeros_like(halo)

    @pl.when(me > 0)
    def _():
        halo_copy(me).wait_recv()
        halo[...] = halo_in[...].astype(jnp.float32)

    upper = lax.broadcasted_iota(jnp.int32, (SUB, LANES), 0) < SUB - 1

    def featured(block, part):
        cols = columns(block, part)
        taps = taps_ref[:, cols].astype(jnp.float32)
        at = 2 * (part * (width // LANES) + block)
        head = jnp.where(upper, halo[pl.ds(at, 1), :], halo[pl.ds(at + 1, 1), :])
        rows = jnp.concatenate([head, proj[:, cols].astype(jnp.float32)], 0)
        total = None
        for tap in range(taps.shape[0]):
            start = SUB - tap
            term = taps[tap:tap + 1] * rows[start:start + tok]
            total = term if total is None else total + term
        return total

    def make_gate(block):
        rounded = (featured(block, 1) * featured(block, 2)).astype(jnp.bfloat16)
        gated[block] = rounded
        return packed(rounded.astype(jnp.float32))

    def start_gate(to, number):
        gate_out[0, number], gate_out[1, number] = make_gate(number)
        send_gate(0, to, number)

    each_partner(start_gate)
    gate_in[0, me], gate_in[1, me] = make_gate(me)
    each_partner(lambda to, number: send_filter(1, to, number))

    left = lax.broadcasted_iota(jnp.int32, (half_tok, LANES), 1) < HALF
    for freq in range(freqs):
        for part in range(2):
            column = turn_ref[part][:, freq:freq + 1]
            turn[freq, part] = jnp.where(left, column[:half_tok], column[half_tok:])
    first[quads - 1] = jnp.zeros(first.shape[1:], first.dtype)

    def spot(tile, shift):
        return pl.ds(pl.multiple_of(shift + tile * ROWS, ROWS), ROWS)

    def pair_lanes(pair):
        return pair // 2, slice((pair % 2) * LANES, (pair % 2 + 1) * LANES)

    def first_section(source, half):
        def run(tile):
            rows = spot(tile, 0)
            spec = forward64([source[half, b, rows, :].astype(jnp.float32) for b in range(n)])

            def turned(freq):
                cos, sin = turn[freq, 0, rows, :], turn[freq, 1, rows, :]
                z = spec[freq]
                if z.im is None:
                    return z.re * cos, -(z.re * sin)
                return z.re * cos + z.im * sin, z.im * cos - z.re * sin

            for pair in range((freqs + 1) // 2):
                even = turned(2 * pair)
                odd = turned(2 * pair + 1) if 2 * pair + 1 < freqs else even
                quad, lanes = pair_lanes(pair)
                for part in range(2):
                    low, high = swapped_halves(even[part], odd[part])
                    first[quad, spot(tile, part * tok), lanes] = low.astype(jnp.bfloat16)
                    first[quad, spot(tile, part * tok + half_tok), lanes] = high.astype(jnp.bfloat16)
        loop(half_tok // ROWS, run)

    def spectrum(quad):
        return jnp.dot(fwd_ref[...], first[quad], preferred_element_type=jnp.float32)

    def filter_section(half):
        first_section(filt_in, half)
        for quad in range(quads):
            fspec[quad] = spectrum(quad)

    def signal_section(half):
        first_section(gate_in, half)
        for quad in range(quads):
            spec = spectrum(quad)
            sr, si = spec[:tok], spec[tok:]
            fr, fi = fspec[quad, :tok], fspec[quad, tok:]
            product = jnp.concatenate([sr * fr - si * fi, sr * fi + si * fr], 0).astype(jnp.bfloat16)
            back[quad] = jnp.dot(bwd_ref[...], product, preferred_element_type=jnp.float32)

    scale = 1.0 / (2 * n * tok)

    def last_section(half):
        def run(tile):
            rows = spot(tile, 0)
            spec = []
            for pair in range((freqs + 1) // 2):
                quad, lanes = pair_lanes(pair)
                parts = [
                    swapped_halves(
                        back[quad, spot(tile, part * tok), lanes],
                        back[quad, spot(tile, part * tok + half_tok), lanes])
                    for part in range(2)
                ]
                for odd in range(2):
                    freq = 2 * pair + odd
                    if freq < freqs:
                        re, im = parts[0][odd], parts[1][odd]
                        cos, sin = turn[freq, 0, rows, :], turn[freq, 1, rows, :]
                        spec.append(Cx(re * cos - im * sin, im * cos + re * sin))
            done = backward64(spec)
            for b in range(n):
                conv_out[half, b, rows, :] = (done[b] * scale).astype(jnp.bfloat16)
        loop(half_tok // ROWS, run)

    wait_all(filt_in, f_sems, 1, 0)
    each_partner(lambda to, number: send_gate(1, to, number))
    filter_section(0)
    wait_all(gate_in, g_sems, 1, 0)
    signal_section(0)
    last_section(0)
    each_partner(lambda to, number: send_conv(0, to, number))

    def ask(block):
        query[block] = featured(block, 0)

    loop(n, ask)

    wait_all(filt_in, f_sems, 1, 1)
    filter_section(1)
    wait_all(gate_in, g_sems, 1, 1)
    signal_section(1)
    last_section(1)
    each_partner(lambda to, number: send_conv(1, to, number))

    for half in range(2):
        conv_in[half, me] = conv_out[half, me]
        wait_all(conv_in, y_sems, 1, half)

    def finish(block):
        cols = columns(block)
        rows = jnp.concatenate(swapped_halves(
            conv_in[0, block].astype(jnp.float32), conv_in[1, block].astype(jnp.float32)), 0)
        mixed = query[block] * (rows + skip_ref[:, cols] * gated[block].astype(jnp.float32))
        out_ref[:, cols] = mixed.astype(jnp.bfloat16)

    loop(n, finish)

    @pl.when(me < n - 1)
    def _():
        halo_copy(me + 1).wait_send()

    for half in range(2):
        wait_all(filt_out, f_sems, 0, half)
        wait_all(gate_out, g_sems, 0, half)
        wait_all(conv_out, y_sems, 0, half)


def cosines(rows, cols, length):
    angle = (np.arange(rows)[:, None] * np.arange(cols)[None, :] % length) * (TWO_PI / length)
    return np.cos(angle), np.sin(angle)


def by_channels(projected, short_filter, long_filter, skip):
    n_inner = lax.axis_size("inner")
    n = lax.axis_size("outer") * n_inner
    tok, width = long_filter.shape
    freqs = n + 1
    cos, sin = cosines(tok, tok, tok)
    forward = np.block([[cos, sin], [-sin, cos]]).astype(jnp.bfloat16)
    backward = np.block([[cos, -sin], [sin, cos]]).astype(jnp.bfloat16)
    turns = np.stack(cosines(tok, LANES, 2 * n * tok)).astype(np.float32)
    vmem = pl.BlockSpec(memory_space=pltpu.VMEM)
    hbm = pl.BlockSpec(memory_space=pl.ANY)
    quads = -(-freqs // 4)
    edges = 2 * projected.shape[1] // LANES
    chunks = pltpu.VMEM((2, n, tok // 2, LANES), jnp.bfloat16)
    dma = pltpu.SemaphoreType.DMA
    return pl.pallas_call(
        functools.partial(kernel, n, n_inner),
        out_shape=jax.ShapeDtypeStruct((tok, width), jnp.bfloat16),
        in_specs=[hbm, hbm] + [vmem] * 5,
        out_specs=vmem,
        scratch_shapes=[
            pltpu.VMEM(projected.shape, jnp.bfloat16),
            pltpu.VMEM(long_filter.shape, jnp.bfloat16),
            pltpu.VMEM((edges, LANES), jnp.float32),
            pltpu.VMEM((edges, LANES), jnp.bfloat16),
            pltpu.VMEM((edges, LANES), jnp.bfloat16),
            chunks, chunks, chunks, chunks, chunks, chunks,
            pltpu.VMEM((n, tok, LANES), jnp.bfloat16),
            pltpu.VMEM((quads, 2 * tok, 4 * HALF), jnp.bfloat16),
            pltpu.VMEM((quads, 2 * tok, 4 * HALF), jnp.float32),
            pltpu.VMEM((quads, 2 * tok, 4 * HALF), jnp.float32),
            pltpu.VMEM((freqs, 2, tok // 2, LANES), jnp.float32),
            pltpu.VMEM((n, tok, LANES), jnp.float32),
            dma, dma, dma, dma,
            dma((2, 2)), dma((2, 2)), dma((2, 2)),
        ],
        compiler_params=pltpu.CompilerParams(
            collective_id=0, has_side_effects=True, vmem_limit_bytes=56 * 1024 * 1024),
        cost_estimate=pl.CostEstimate(
            flops=2 * 3 * freqs * (2 * tok) ** 2 * LANES,
            bytes_accessed=10 * tok * width, transcendentals=0),
    )(projected, long_filter, short_filter, skip[None, :],
      jnp.asarray(forward), jnp.asarray(backward), jnp.asarray(turns))


def passed_along(value, axis, by):
    length = lax.axis_size(axis)
    pairs = [(i, i + by) for i in range(length) if 0 <= i + by < length]
    return lax.ppermute(value, axis, pairs)


def turn_table(rows, cols, length):
    product = rows * cols % length
    angle = product.astype(jnp.float32) * (TWO_PI / length)
    return (jnp.cos(angle), jnp.sin(angle))


def counting(count):
    return jnp.arange(count, dtype=jnp.int32)


def narrowed(table_pair):
    return (table_pair[0].astype(jnp.bfloat16), table_pair[1].astype(jnp.bfloat16))


def contract(form, table, values):
    return jnp.einsum(form, table, values, preferred_element_type=jnp.float32)


def shards(projected, short_filter, long_filter, skip):
    outer_count = lax.axis_size("outer")
    inner_count = lax.axis_size("inner")
    segments = outer_count * inner_count
    tok_rows, width_cols = long_filter.shape
    local_rows = tok_rows // segments
    freq_rows = 2 * segments
    freq_local = 2
    transform = freq_rows * tok_rows
    position = lax.axis_index(("outer", "inner"))
    tap_count = short_filter.shape[0]
    rim_count = tap_count - 1
    previous_rows = passed_along(projected[tok_rows - rim_count :], ("outer", "inner"), 1)
    extended = jnp.concatenate([previous_rows, projected], 0)
    featured = jnp.zeros(projected.shape, jnp.float32)
    for tap_index in range(tap_count):
        offset = rim_count - tap_index
        featured = featured + short_filter[tap_index].astype(jnp.float32) * extended[
            offset : offset + tok_rows
        ].astype(jnp.float32)
    query_rows = featured[:, :width_cols]
    gated_rows = (featured[:, width_cols : 2 * width_cols] * featured[:, 2 * width_cols :]).astype(
        jnp.bfloat16
    )
    cos_first, sin_first = narrowed(
        turn_table(counting(freq_rows)[:, None], counting(segments)[None, :], freq_rows)
    )
    owned_rows = position * local_rows + counting(local_rows)
    turn_cos, turn_sin = turn_table(counting(freq_rows)[:, None], owned_rows[None, :], transform)
    turn_cos = turn_cos[:, :, None]
    turn_sin = turn_sin[:, :, None]
    cos_local, sin_local = narrowed(
        turn_table(counting(tok_rows)[:, None], counting(tok_rows)[None, :], tok_rows)
    )
    owned_freqs = position * freq_local + counting(freq_local)
    back_cos, back_sin = turn_table(owned_freqs[:, None], counting(tok_rows)[None, :], transform)
    back_cos = back_cos[:, :, None]
    back_sin = back_sin[:, :, None]
    cos_last, sin_last = narrowed(
        turn_table(counting(segments)[:, None], counting(freq_rows)[None, :], freq_rows)
    )

    def first_section(stacked):
        real_part = contract("kb,bac->kac", cos_first, stacked)
        imag_part = -contract("kb,bac->kac", sin_first, stacked)
        out_real = (real_part * turn_cos + imag_part * turn_sin).astype(jnp.bfloat16)
        out_imag = (imag_part * turn_cos - real_part * turn_sin).astype(jnp.bfloat16)
        return (out_real, out_imag)

    def forward_local(real_half, imag_half):
        spec_real = contract("ua,kac->kuc", cos_local, real_half) + contract(
            "ua,kac->kuc", sin_local, imag_half
        )
        spec_imag = contract("ua,kac->kuc", cos_local, imag_half) - contract(
            "ua,kac->kuc", sin_local, real_half
        )
        return (spec_real, spec_imag)

    moved = (
        lax.all_to_all(
            gated_rows.reshape(segments, local_rows, width_cols),
            ("outer", "inner"),
            split_axis=0,
            concat_axis=0,
            tiled=True,
        ),
        lax.all_to_all(
            long_filter.reshape(segments, local_rows, width_cols),
            ("outer", "inner"),
            split_axis=0,
            concat_axis=0,
            tiled=True,
        ),
    )
    signal_cols = moved[0]
    filter_cols = moved[1]
    signal_real, signal_imag = first_section(signal_cols)
    filter_real, filter_imag = first_section(filter_cols)
    spectral_pieces = (
        lax.all_to_all(signal_real, ("outer", "inner"), split_axis=0, concat_axis=1, tiled=True),
        lax.all_to_all(signal_imag, ("outer", "inner"), split_axis=0, concat_axis=1, tiled=True),
        lax.all_to_all(filter_real, ("outer", "inner"), split_axis=0, concat_axis=1, tiled=True),
        lax.all_to_all(filter_imag, ("outer", "inner"), split_axis=0, concat_axis=1, tiled=True),
    )
    signal_real, signal_imag = forward_local(spectral_pieces[0], spectral_pieces[1])
    filter_real, filter_imag = forward_local(spectral_pieces[2], spectral_pieces[3])
    product_real = (signal_real * filter_real - signal_imag * filter_imag).astype(jnp.bfloat16)
    product_imag = (signal_real * filter_imag + signal_imag * filter_real).astype(jnp.bfloat16)
    back_real = contract("au,kuc->kac", cos_local, product_real) - contract(
        "au,kuc->kac", sin_local, product_imag
    )
    back_imag = contract("au,kuc->kac", cos_local, product_imag) + contract(
        "au,kuc->kac", sin_local, product_real
    )
    out_real = (back_real * back_cos - back_imag * back_sin).astype(jnp.bfloat16)
    out_imag = (back_imag * back_cos + back_real * back_sin).astype(jnp.bfloat16)
    moved = (
        lax.all_to_all(out_real, ("outer", "inner"), split_axis=1, concat_axis=0, tiled=True),
        lax.all_to_all(out_imag, ("outer", "inner"), split_axis=1, concat_axis=0, tiled=True),
    )
    rows_real = moved[0]
    rows_imag = moved[1]
    long_conv = (
        contract("bk,kac->bac", cos_last, rows_real) - contract("bk,kac->bac", sin_last, rows_imag)
    ) * (1.0 / transform)
    moved = lax.all_to_all(
        long_conv.astype(jnp.bfloat16), ("outer", "inner"), split_axis=0, concat_axis=0, tiled=True
    )
    conv_rows = moved.reshape(tok_rows, width_cols)
    mixed = query_rows * (
        conv_rows.astype(jnp.float32) + skip[None, :] * gated_rows.astype(jnp.float32)
    )
    return mixed.astype(jnp.bfloat16)


def operator(projected, short_filter, long_filter, skip):
    segments = lax.axis_size("outer") * lax.axis_size("inner")
    tok_rows, width_cols = long_filter.shape
    if 2 * segments == RADIX * RADIX and tok_rows == LANES and width_cols == segments * LANES:
        return by_channels(projected, short_filter, long_filter, skip)
    return shards(projected, short_filter, long_filter, skip)


def solution(mesh):
    in_specs = (P(("outer", "inner"), None), P(), P(("outer", "inner"), None), P())
    out_specs = P(("outer", "inner"), None)
    return jax.shard_map(operator, mesh=mesh, in_specs=in_specs, out_specs=out_specs, check_vma=False)
```

```python
import functools
import math

import jax
import jax.numpy as jnp
import numpy as np
from jax import lax
from jax.experimental import pallas as pl
from jax.experimental.pallas import tpu as pltpu
from jax.sharding import PartitionSpec as P

TWO_PI = 2.0 * math.pi
MESH = pl.DeviceIdType.MESH
LANES = 128
HALF = LANES // 2
ROWS = 16
SUB = 8
RADIX = 8


class Cx:
    def __init__(self, re, im=None):
        self.re, self.im = re, im

    def __add__(self, other):
        if self.im is None:
            im = other.im
        elif other.im is None:
            im = self.im
        else:
            im = self.im + other.im
        return Cx(self.re + other.re, im)

    def __sub__(self, other):
        if other.im is None:
            im = self.im
        elif self.im is None:
            im = -other.im
        else:
            im = self.im - other.im
        return Cx(self.re - other.re, im)

    def conj(self):
        return Cx(self.re, None if self.im is None else -self.im)

    def times(self, turns, length):
        turns = turns % length
        if turns == 0:
            return self
        if 2 * turns == length:
            return Cx(-self.re, None if self.im is None else -self.im)
        cos, sin = math.cos(TWO_PI * turns / length), math.sin(TWO_PI * turns / length)
        if self.im is None:
            return Cx(self.re * cos, self.re * sin)
        if 8 * turns % length == 0 and 4 * turns % length != 0:
            half = math.sqrt(0.5)
            one, two = self.re * half, self.im * half
            signs = (round(cos / half), round(sin / half))
            re = {(1, 1): one - two, (1, -1): one + two, (-1, 1): -(one + two), (-1, -1): two - one}
            im = {(1, 1): one + two, (1, -1): two - one, (-1, 1): one - two, (-1, -1): -(one + two)}
            return Cx(re[signs], im[signs])
        return Cx(self.re * cos - self.im * sin, self.re * sin + self.im * cos)

    def plus_i(self, other, sign):
        if other.im is None:
            re = self.re
        else:
            re = self.re - other.im if sign > 0 else self.re + other.im
        turned = other.re if sign > 0 else -other.re
        return Cx(re, turned if self.im is None else self.im + turned)


def dft4(z, sign):
    s, t, u, v = z[0] + z[2], z[0] - z[2], z[1] + z[3], z[1] - z[3]
    return [s + u, t.plus_i(v, sign), s - u, t.plus_i(v, -sign)]


def dft8(z, sign):
    even, odd = dft4(z[0::2], sign), dft4(z[1::2], sign)
    out = [None] * 8
    for k in range(4):
        if k == 2:
            out[2], out[6] = even[2].plus_i(odd[2], sign), even[2].plus_i(odd[2], -sign)
        else:
            turned = odd[k].times(sign * k, 8)
            out[k], out[k + 4] = even[k] + turned, even[k] - turned
    return out


def forward64(x):
    half = math.sqrt(0.5)
    first = [[None] * 8 for _ in range(5)]
    for b in range(8):
        x0, x1, x2, x3 = x[b], x[b + 8], x[b + 16], x[b + 24]
        p, q, d = x0 + x2, x1 + x3, x1 - x3
        e, f = q * half, d * half
        first[0][b] = Cx(p + q)
        first[4][b] = Cx(p - q)
        first[2][b] = Cx(x0 - x2, -d)
        first[1][b] = Cx(x0 + f, -(e + x2))
        first[3][b] = Cx(x0 - f, x2 - e)
    out = {}
    for k1 in range(5):
        done = dft8([first[k1][b].times(-b * k1, 64) for b in range(8)], -1)
        for k0 in range(8):
            freq = k1 + 8 * k0
            if freq <= 32:
                out[freq] = done[k0]
            elif k1 not in (0, 4):
                out[64 - freq] = done[k0].conj()
    return out


def backward64(spec):
    half = math.sqrt(0.5)
    held = [None] * 5
    for k1 in range(5):
        values = []
        for k0 in range(8):
            freq = k1 + 8 * k0
            values.append(spec[freq] if freq <= 32 else spec[64 - freq].conj())
        done = dft8(values, 1)
        held[k1] = [done[b].times(b * k1, 64) for b in range(8)]
    out = [None] * 32
    for b in range(8):
        h0, h4 = held[0][b].re, held[4][b].re
        h1, h2, h3 = held[1][b], held[2][b], held[3][b]
        plus, minus = h0 + h4, h0 - h4
        a1, a3 = (h1.re - h3.re), (h1.im + h3.im)
        out[b] = plus + 2.0 * (h1.re + h2.re + h3.re)
        out[b + 16] = plus + 2.0 * (h3.im - h1.im - h2.re)
        out[b + 8] = minus + 2.0 * (half * (a1 - a3) - h2.im)
        out[b + 24] = minus + 2.0 * (h2.im - half * (a1 + a3))
    return out


def swapped_halves(x, y):
    left = lax.broadcasted_iota(jnp.int32, x.shape, 1) < HALF
    return (
        jnp.where(left, x, pltpu.roll(y, HALF, 1)),
        jnp.where(left, pltpu.roll(x, HALF, 1), y),
    )


def kernel(
    n, n_inner, proj_hbm, filt_hbm, taps_ref, skip_ref, fwd_ref, bwd_ref, turn_ref, out_ref,
    proj, filt, halo, halo_out, halo_in, filt_out, gate_out, conv_out, filt_in, gate_in, conv_in,
    gated, first, fspec, back, turn, query, direct, tail,
    tail_sem, proj_sem, filt_sem, halo_send, halo_recv, f_sems, g_sems, y_sems,
):
    tok, width = filt.shape
    freqs = n + 1
    half_tok = tok // 2
    quads = first.shape[0]
    outer, inner = lax.axis_index("outer"), lax.axis_index("inner")
    me = outer * n_inner + inner

    def columns(block, part=0):
        return pl.ds(pl.multiple_of(part * width + block * LANES, LANES), LANES)

    n_z = n_inner // 2
    n_x = n // n_inner // 2
    x, core = lax.div(outer, 2), lax.rem(outer, 2)
    z, y = lax.div(inner, 2), lax.rem(inner, 2)

    def partner(step):
        turn_of = lax.div(step, n_z)
        to_z = lax.rem(z + step + (n_z // 2) * core, n_z)
        to_x = lax.rem(x + turn_of + y, n_x)
        to_y = lax.rem(y + lax.div(turn_of, n_x) + core, 2)
        to_core = lax.rem(core + lax.div(turn_of, 2 * n_x), 2)
        to = (to_x * 2 + to_core, to_z * 2 + to_y)
        return to, to[0] * n_inner + to[1]

    def each_partner(body):
        def run(step, carry):
            to, number = partner(step)

            @pl.when(number != me)
            def _():
                body(to, number)
            return carry
        lax.fori_loop(0, n, run, 0)

    def loop(count, body):
        def run(step, carry):
            body(step)
            return carry
        lax.fori_loop(0, count, run, 0)

    def halo_copy(to):
        return pltpu.make_async_remote_copy(
            src_ref=halo_out, dst_ref=halo_in, send_sem=halo_send, recv_sem=halo_recv,
            device_id=(lax.div(to, n_inner), lax.rem(to, n_inner)), device_id_type=MESH,
        )

    def send(source, target, sems, half, to, number):
        pltpu.make_async_remote_copy(
            src_ref=source.at[half, number], dst_ref=target.at[half, me],
            send_sem=sems.at[0, half], recv_sem=sems.at[1, half],
            device_id=to, device_id_type=MESH,
        ).start()

    def wait_all(buffer, sems, way, half):
        chunks = buffer.at[half, pl.ds(0, n - 1)]
        pltpu.make_async_copy(chunks, chunks, sems.at[way, half]).wait()

    send_filter = functools.partial(send, filt_out, filt_in, f_sems)
    send_gate = functools.partial(send, gate_out, gate_in, g_sems)
    send_conv = functools.partial(send, conv_out, conv_in, y_sems)

    load_tail = pltpu.make_async_copy(
        proj_hbm.at[pl.ds(tok - ROWS, ROWS), :], tail, tail_sem)
    load_tail.start()
    load_filt = pltpu.make_async_copy(filt_hbm, filt, filt_sem)
    load_filt.start()
    load = pltpu.make_async_copy(proj_hbm, proj, proj_sem)
    load.start()

    barrier = pltpu.get_barrier_semaphore()
    each_partner(lambda to, number: pl.semaphore_signal(
        barrier, inc=1, device_id=to, device_id_type=MESH))

    load_tail.wait()
    blocks = proj.shape[1] // LANES
    for block in range(blocks):
        last = tail[:, block * LANES:(block + 1) * LANES].astype(jnp.float32)
        halo[2 * block:2 * block + 2, :] = last[ROWS - 2:]
    halo_out[...] = halo[...].astype(jnp.bfloat16)

    load_filt.wait()
    pl.semaphore_wait(barrier, n - 1)

    @pl.when(me < n - 1)
    def _():
        halo_copy(me + 1).start()

    def packed(values):
        first_half, second_half = swapped_halves(values[:half_tok], values[half_tok:])
        return first_half.astype(jnp.bfloat16), second_half.astype(jnp.bfloat16)

    def pack_filter(block):
        return packed(filt[:, columns(block)].astype(jnp.float32))

    def start_filter(to, number):
        filt_out[0, number], filt_out[1, number] = pack_filter(number)
        send_filter(0, to, number)

    each_partner(start_filter)
    filt_in[0, me], filt_in[1, me] = pack_filter(me)

    load.wait()

    @pl.when(me == 0)
    def _():
        halo[...] = jnp.zeros_like(halo)

    @pl.when(me > 0)
    def _():
        halo_copy(me).wait_recv()
        halo[...] = halo_in[...].astype(jnp.float32)

    upper = lax.broadcasted_iota(jnp.int32, (SUB, LANES), 0) < SUB - 1

    def featured(block, part):
        cols = columns(block, part)
        taps = taps_ref[:, cols].astype(jnp.float32)
        at = 2 * (part * (width // LANES) + block)
        head = jnp.where(upper, halo[pl.ds(at, 1), :], halo[pl.ds(at + 1, 1), :])
        rows = jnp.concatenate([head, proj[:, cols].astype(jnp.float32)], 0)
        total = None
        for tap in range(taps.shape[0]):
            start = SUB - tap
            term = taps[tap:tap + 1] * rows[start:start + tok]
            total = term if total is None else total + term
        return total

    def make_gate(block):
        rounded = (featured(block, 1) * featured(block, 2)).astype(jnp.bfloat16)
        gated[block] = rounded
        return packed(rounded.astype(jnp.float32))

    def start_gate(to, number):
        gate_out[0, number], gate_out[1, number] = make_gate(number)
        send_gate(0, to, number)

    each_partner(start_gate)
    gate_in[0, me], gate_in[1, me] = make_gate(me)
    each_partner(lambda to, number: send_filter(1, to, number))

    left = lax.broadcasted_iota(jnp.int32, (half_tok, LANES), 1) < HALF
    for freq in range(freqs):
        for part in range(2):
            column = turn_ref[part][:, freq:freq + 1]
            turn[freq, part] = jnp.where(left, column[:half_tok], column[half_tok:])
    first[quads - 1] = jnp.zeros(first.shape[1:], first.dtype)

    def spot(tile, shift):
        return pl.ds(pl.multiple_of(shift + tile * ROWS, ROWS), ROWS)

    def pair_lanes(pair):
        return pair // 2, slice((pair % 2) * LANES, (pair % 2 + 1) * LANES)

    def first_section(source, half):
        def run(tile):
            rows = spot(tile, 0)
            spec = forward64([source[half, b, rows, :].astype(jnp.float32) for b in range(n)])

            def turned(freq):
                cos, sin = turn[freq, 0, rows, :], turn[freq, 1, rows, :]
                z = spec[freq]
                if z.im is None:
                    return z.re * cos, -(z.re * sin)
                return z.re * cos + z.im * sin, z.im * cos - z.re * sin

            for pair in range((freqs + 1) // 2):
                even = turned(2 * pair)
                odd = turned(2 * pair + 1) if 2 * pair + 1 < freqs else even
                quad, lanes = pair_lanes(pair)
                for part in range(2):
                    low, high = swapped_halves(even[part], odd[part])
                    first[quad, spot(tile, part * tok), lanes] = low.astype(jnp.bfloat16)
                    first[quad, spot(tile, part * tok + half_tok), lanes] = high.astype(jnp.bfloat16)
        loop(half_tok // ROWS, run)

    def spectrum(quad):
        return jnp.dot(fwd_ref[...], first[quad], preferred_element_type=jnp.float32)

    def filter_section(half):
        first_section(filt_in, half)
        for quad in range(quads):
            fspec[quad] = spectrum(quad)

    def signal_section(half):
        first_section(gate_in, half)
        for quad in range(quads):
            spec = spectrum(quad)
            sr, si = spec[:tok], spec[tok:]
            fr, fi = fspec[quad, :tok], fspec[quad, tok:]
            product = jnp.concatenate([sr * fr - si * fi, sr * fi + si * fr], 0).astype(jnp.bfloat16)
            back[quad] = jnp.dot(bwd_ref[...], product, preferred_element_type=jnp.float32)

    scale = 1.0 / (2 * n * tok)

    def last_section(half):
        def run(tile):
            rows = spot(tile, 0)
            spec = []
            for pair in range((freqs + 1) // 2):
                quad, lanes = pair_lanes(pair)
                parts = [
                    swapped_halves(
                        back[quad, spot(tile, part * tok), lanes],
                        back[quad, spot(tile, part * tok + half_tok), lanes])
                    for part in range(2)
                ]
                for odd in range(2):
                    freq = 2 * pair + odd
                    if freq < freqs:
                        re, im = parts[0][odd], parts[1][odd]
                        cos, sin = turn[freq, 0, rows, :], turn[freq, 1, rows, :]
                        spec.append(Cx(re * cos - im * sin, im * cos + re * sin))
            done = backward64(spec)
            for b in range(n):
                conv_out[half, b, rows, :] = (done[b] * scale).astype(jnp.bfloat16)
        loop(half_tok // ROWS, run)

    wait_all(filt_in, f_sems, 1, 0)
    each_partner(lambda to, number: send_gate(1, to, number))
    filter_section(0)
    wait_all(gate_in, g_sems, 1, 0)
    signal_section(0)
    last_section(0)
    wait_all(filt_in, f_sems, 1, 1)
    filter_section(1)
    wait_all(gate_in, g_sems, 1, 1)
    each_partner(lambda to, number: send_conv(0, to, number))
    signal_section(1)
    last_section(1)
    each_partner(lambda to, number: send_conv(1, to, number))

    def ask(block):
        asked = featured(block, 0)
        query[block] = asked
        direct[block] = asked * (skip_ref[:, columns(block)] * gated[block].astype(jnp.float32))

    loop(n, ask)

    for half in range(2):
        conv_in[half, me] = conv_out[half, me]
        wait_all(conv_in, y_sems, 1, half)

    def finish(block):
        cols = columns(block)
        rows = jnp.concatenate(swapped_halves(
            conv_in[0, block].astype(jnp.float32), conv_in[1, block].astype(jnp.float32)), 0)
        out_ref[:, cols] = (query[block] * rows + direct[block]).astype(jnp.bfloat16)

    loop(n, finish)

    @pl.when(me < n - 1)
    def _():
        halo_copy(me + 1).wait_send()

    for half in range(2):
        wait_all(filt_out, f_sems, 0, half)
        wait_all(gate_out, g_sems, 0, half)
        wait_all(conv_out, y_sems, 0, half)


def cosines(rows, cols, length):
    angle = (np.arange(rows)[:, None] * np.arange(cols)[None, :] % length) * (TWO_PI / length)
    return np.cos(angle), np.sin(angle)


def by_channels(projected, short_filter, long_filter, skip):
    n_inner = lax.axis_size("inner")
    n = lax.axis_size("outer") * n_inner
    tok, width = long_filter.shape
    freqs = n + 1
    cos, sin = cosines(tok, tok, tok)
    forward = np.block([[cos, sin], [-sin, cos]]).astype(jnp.bfloat16)
    backward = np.block([[cos, -sin], [sin, cos]]).astype(jnp.bfloat16)
    turns = np.stack(cosines(tok, LANES, 2 * n * tok)).astype(np.float32)
    vmem = pl.BlockSpec(memory_space=pltpu.VMEM)
    hbm = pl.BlockSpec(memory_space=pl.ANY)
    quads = -(-freqs // 4)
    edges = 2 * projected.shape[1] // LANES
    chunks = pltpu.VMEM((2, n, tok // 2, LANES), jnp.bfloat16)
    dma = pltpu.SemaphoreType.DMA
    return pl.pallas_call(
        functools.partial(kernel, n, n_inner),
        out_shape=jax.ShapeDtypeStruct((tok, width), jnp.bfloat16),
        in_specs=[hbm, hbm] + [vmem] * 5,
        out_specs=vmem,
        scratch_shapes=[
            pltpu.VMEM(projected.shape, jnp.bfloat16),
            pltpu.VMEM(long_filter.shape, jnp.bfloat16),
            pltpu.VMEM((edges, LANES), jnp.float32),
            pltpu.VMEM((edges, LANES), jnp.bfloat16),
            pltpu.VMEM((edges, LANES), jnp.bfloat16),
            chunks, chunks, chunks, chunks, chunks, chunks,
            pltpu.VMEM((n, tok, LANES), jnp.bfloat16),
            pltpu.VMEM((quads, 2 * tok, 4 * HALF), jnp.bfloat16),
            pltpu.VMEM((quads, 2 * tok, 4 * HALF), jnp.float32),
            pltpu.VMEM((quads, 2 * tok, 4 * HALF), jnp.float32),
            pltpu.VMEM((freqs, 2, tok // 2, LANES), jnp.float32),
            pltpu.VMEM((n, tok, LANES), jnp.float32),
            pltpu.VMEM((n, tok, LANES), jnp.float32),
            pltpu.VMEM((ROWS, projected.shape[1]), jnp.bfloat16),
            dma, dma, dma, dma, dma,
            dma((2, 2)), dma((2, 2)), dma((2, 2)),
        ],
        compiler_params=pltpu.CompilerParams(
            collective_id=0, has_side_effects=True, vmem_limit_bytes=56 * 1024 * 1024),
        cost_estimate=pl.CostEstimate(
            flops=2 * 3 * freqs * (2 * tok) ** 2 * LANES,
            bytes_accessed=10 * tok * width, transcendentals=0),
    )(projected, long_filter, short_filter, skip[None, :],
      jnp.asarray(forward), jnp.asarray(backward), jnp.asarray(turns))


def passed_along(value, axis, by):
    length = lax.axis_size(axis)
    pairs = [(i, i + by) for i in range(length) if 0 <= i + by < length]
    return lax.ppermute(value, axis, pairs)


def turn_table(rows, cols, length):
    product = rows * cols % length
    angle = product.astype(jnp.float32) * (TWO_PI / length)
    return (jnp.cos(angle), jnp.sin(angle))


def counting(count):
    return jnp.arange(count, dtype=jnp.int32)


def narrowed(table_pair):
    return (table_pair[0].astype(jnp.bfloat16), table_pair[1].astype(jnp.bfloat16))


def contract(form, table, values):
    return jnp.einsum(form, table, values, preferred_element_type=jnp.float32)


def shards(projected, short_filter, long_filter, skip):
    outer_count = lax.axis_size("outer")
    inner_count = lax.axis_size("inner")
    segments = outer_count * inner_count
    tok_rows, width_cols = long_filter.shape
    local_rows = tok_rows // segments
    freq_rows = 2 * segments
    freq_local = 2
    transform = freq_rows * tok_rows
    position = lax.axis_index(("outer", "inner"))
    tap_count = short_filter.shape[0]
    rim_count = tap_count - 1
    previous_rows = passed_along(projected[tok_rows - rim_count :], ("outer", "inner"), 1)
    extended = jnp.concatenate([previous_rows, projected], 0)
    featured = jnp.zeros(projected.shape, jnp.float32)
    for tap_index in range(tap_count):
        offset = rim_count - tap_index
        featured = featured + short_filter[tap_index].astype(jnp.float32) * extended[
            offset : offset + tok_rows
        ].astype(jnp.float32)
    query_rows = featured[:, :width_cols]
    gated_rows = (featured[:, width_cols : 2 * width_cols] * featured[:, 2 * width_cols :]).astype(
        jnp.bfloat16
    )
    cos_first, sin_first = narrowed(
        turn_table(counting(freq_rows)[:, None], counting(segments)[None, :], freq_rows)
    )
    owned_rows = position * local_rows + counting(local_rows)
    turn_cos, turn_sin = turn_table(counting(freq_rows)[:, None], owned_rows[None, :], transform)
    turn_cos = turn_cos[:, :, None]
    turn_sin = turn_sin[:, :, None]
    cos_local, sin_local = narrowed(
        turn_table(counting(tok_rows)[:, None], counting(tok_rows)[None, :], tok_rows)
    )
    owned_freqs = position * freq_local + counting(freq_local)
    back_cos, back_sin = turn_table(owned_freqs[:, None], counting(tok_rows)[None, :], transform)
    back_cos = back_cos[:, :, None]
    back_sin = back_sin[:, :, None]
    cos_last, sin_last = narrowed(
        turn_table(counting(segments)[:, None], counting(freq_rows)[None, :], freq_rows)
    )

    def first_section(stacked):
        real_part = contract("kb,bac->kac", cos_first, stacked)
        imag_part = -contract("kb,bac->kac", sin_first, stacked)
        out_real = (real_part * turn_cos + imag_part * turn_sin).astype(jnp.bfloat16)
        out_imag = (imag_part * turn_cos - real_part * turn_sin).astype(jnp.bfloat16)
        return (out_real, out_imag)

    def forward_local(real_half, imag_half):
        spec_real = contract("ua,kac->kuc", cos_local, real_half) + contract(
            "ua,kac->kuc", sin_local, imag_half
        )
        spec_imag = contract("ua,kac->kuc", cos_local, imag_half) - contract(
            "ua,kac->kuc", sin_local, real_half
        )
        return (spec_real, spec_imag)

    moved = (
        lax.all_to_all(
            gated_rows.reshape(segments, local_rows, width_cols),
            ("outer", "inner"),
            split_axis=0,
            concat_axis=0,
            tiled=True,
        ),
        lax.all_to_all(
            long_filter.reshape(segments, local_rows, width_cols),
            ("outer", "inner"),
            split_axis=0,
            concat_axis=0,
            tiled=True,
        ),
    )
    signal_cols = moved[0]
    filter_cols = moved[1]
    signal_real, signal_imag = first_section(signal_cols)
    filter_real, filter_imag = first_section(filter_cols)
    spectral_pieces = (
        lax.all_to_all(signal_real, ("outer", "inner"), split_axis=0, concat_axis=1, tiled=True),
        lax.all_to_all(signal_imag, ("outer", "inner"), split_axis=0, concat_axis=1, tiled=True),
        lax.all_to_all(filter_real, ("outer", "inner"), split_axis=0, concat_axis=1, tiled=True),
        lax.all_to_all(filter_imag, ("outer", "inner"), split_axis=0, concat_axis=1, tiled=True),
    )
    signal_real, signal_imag = forward_local(spectral_pieces[0], spectral_pieces[1])
    filter_real, filter_imag = forward_local(spectral_pieces[2], spectral_pieces[3])
    product_real = (signal_real * filter_real - signal_imag * filter_imag).astype(jnp.bfloat16)
    product_imag = (signal_real * filter_imag + signal_imag * filter_real).astype(jnp.bfloat16)
    back_real = contract("au,kuc->kac", cos_local, product_real) - contract(
        "au,kuc->kac", sin_local, product_imag
    )
    back_imag = contract("au,kuc->kac", cos_local, product_imag) + contract(
        "au,kuc->kac", sin_local, product_real
    )
    out_real = (back_real * back_cos - back_imag * back_sin).astype(jnp.bfloat16)
    out_imag = (back_imag * back_cos + back_real * back_sin).astype(jnp.bfloat16)
    moved = (
        lax.all_to_all(out_real, ("outer", "inner"), split_axis=1, concat_axis=0, tiled=True),
        lax.all_to_all(out_imag, ("outer", "inner"), split_axis=1, concat_axis=0, tiled=True),
    )
    rows_real = moved[0]
    rows_imag = moved[1]
    long_conv = (
        contract("bk,kac->bac", cos_last, rows_real) - contract("bk,kac->bac", sin_last, rows_imag)
    ) * (1.0 / transform)
    moved = lax.all_to_all(
        long_conv.astype(jnp.bfloat16), ("outer", "inner"), split_axis=0, concat_axis=0, tiled=True
    )
    conv_rows = moved.reshape(tok_rows, width_cols)
    mixed = query_rows * (
        conv_rows.astype(jnp.float32) + skip[None, :] * gated_rows.astype(jnp.float32)
    )
    return mixed.astype(jnp.bfloat16)


def operator(projected, short_filter, long_filter, skip):
    segments = lax.axis_size("outer") * lax.axis_size("inner")
    tok_rows, width_cols = long_filter.shape
    if 2 * segments == RADIX * RADIX and tok_rows == LANES and width_cols == segments * LANES:
        return by_channels(projected, short_filter, long_filter, skip)
    return shards(projected, short_filter, long_filter, skip)


def solution(mesh):
    in_specs = (P(("outer", "inner"), None), P(), P(("outer", "inner"), None), P())
    out_specs = P(("outer", "inner"), None)
    return jax.shard_map(operator, mesh=mesh, in_specs=in_specs, out_specs=out_specs, check_vma=False)
```

```python
import functools
import math

import jax
import jax.numpy as jnp
import numpy as np
from jax import lax
from jax.experimental import pallas as pl
from jax.experimental.pallas import tpu as pltpu
from jax.sharding import PartitionSpec as P

TWO_PI = 2.0 * math.pi
MESH = pl.DeviceIdType.MESH
LANES = 128
HALF = LANES // 2
ROWS = 16
SUB = 8
RADIX = 8


class Cx:
    def __init__(self, re, im=None):
        self.re, self.im = re, im

    def __add__(self, other):
        if self.im is None:
            im = other.im
        elif other.im is None:
            im = self.im
        else:
            im = self.im + other.im
        return Cx(self.re + other.re, im)

    def __sub__(self, other):
        if other.im is None:
            im = self.im
        elif self.im is None:
            im = -other.im
        else:
            im = self.im - other.im
        return Cx(self.re - other.re, im)

    def conj(self):
        return Cx(self.re, None if self.im is None else -self.im)

    def times(self, turns, length):
        turns = turns % length
        if turns == 0:
            return self
        if 2 * turns == length:
            return Cx(-self.re, None if self.im is None else -self.im)
        cos, sin = math.cos(TWO_PI * turns / length), math.sin(TWO_PI * turns / length)
        if self.im is None:
            return Cx(self.re * cos, self.re * sin)
        if 8 * turns % length == 0 and 4 * turns % length != 0:
            half = math.sqrt(0.5)
            one, two = self.re * half, self.im * half
            signs = (round(cos / half), round(sin / half))
            re = {(1, 1): one - two, (1, -1): one + two, (-1, 1): -(one + two), (-1, -1): two - one}
            im = {(1, 1): one + two, (1, -1): two - one, (-1, 1): one - two, (-1, -1): -(one + two)}
            return Cx(re[signs], im[signs])
        return Cx(self.re * cos - self.im * sin, self.re * sin + self.im * cos)

    def plus_i(self, other, sign):
        if other.im is None:
            re = self.re
        else:
            re = self.re - other.im if sign > 0 else self.re + other.im
        turned = other.re if sign > 0 else -other.re
        return Cx(re, turned if self.im is None else self.im + turned)


def dft4(z, sign):
    s, t, u, v = z[0] + z[2], z[0] - z[2], z[1] + z[3], z[1] - z[3]
    return [s + u, t.plus_i(v, sign), s - u, t.plus_i(v, -sign)]


def dft8(z, sign):
    even, odd = dft4(z[0::2], sign), dft4(z[1::2], sign)
    out = [None] * 8
    for k in range(4):
        if k == 2:
            out[2], out[6] = even[2].plus_i(odd[2], sign), even[2].plus_i(odd[2], -sign)
        else:
            turned = odd[k].times(sign * k, 8)
            out[k], out[k + 4] = even[k] + turned, even[k] - turned
    return out


def forward64(x):
    half = math.sqrt(0.5)
    first = [[None] * 8 for _ in range(5)]
    for b in range(8):
        x0, x1, x2, x3 = x[b], x[b + 8], x[b + 16], x[b + 24]
        p, q, d = x0 + x2, x1 + x3, x1 - x3
        e, f = q * half, d * half
        first[0][b] = Cx(p + q)
        first[4][b] = Cx(p - q)
        first[2][b] = Cx(x0 - x2, -d)
        first[1][b] = Cx(x0 + f, -(e + x2))
        first[3][b] = Cx(x0 - f, x2 - e)
    out = {}
    for k1 in range(5):
        done = dft8([first[k1][b].times(-b * k1, 64) for b in range(8)], -1)
        for k0 in range(8):
            freq = k1 + 8 * k0
            if freq <= 32:
                out[freq] = done[k0]
            elif k1 not in (0, 4):
                out[64 - freq] = done[k0].conj()
    return out


def backward64(spec):
    half = math.sqrt(0.5)
    held = [None] * 5
    for k1 in range(5):
        values = []
        for k0 in range(8):
            freq = k1 + 8 * k0
            values.append(spec[freq] if freq <= 32 else spec[64 - freq].conj())
        done = dft8(values, 1)
        held[k1] = [done[b].times(b * k1, 64) for b in range(8)]
    out = [None] * 32
    for b in range(8):
        h0, h4 = held[0][b].re, held[4][b].re
        h1, h2, h3 = held[1][b], held[2][b], held[3][b]
        plus, minus = h0 + h4, h0 - h4
        a1, a3 = (h1.re - h3.re), (h1.im + h3.im)
        out[b] = plus + 2.0 * (h1.re + h2.re + h3.re)
        out[b + 16] = plus + 2.0 * (h3.im - h1.im - h2.re)
        out[b + 8] = minus + 2.0 * (half * (a1 - a3) - h2.im)
        out[b + 24] = minus + 2.0 * (h2.im - half * (a1 + a3))
    return out


def swapped_halves(x, y):
    left = lax.broadcasted_iota(jnp.int32, x.shape, 1) < HALF
    return (
        jnp.where(left, x, pltpu.roll(y, HALF, 1)),
        jnp.where(left, pltpu.roll(x, HALF, 1), y),
    )


def kernel(
    n, n_inner, proj_hbm, filt_hbm, taps_ref, skip_ref, fwd_ref, bwd_ref, turn_ref, out_ref,
    proj, filt, halo, halo_out, halo_in, filt_out, gate_out, conv_out, filt_in, gate_in, conv_in,
    gated, first, fspec, back, turn, query, direct, tail,
    tail_sem, proj_sem, filt_sem, halo_send, halo_recv, f_sems, g_sems, y_sems,
):
    tok, width = filt.shape
    freqs = n + 1
    half_tok = tok // 2
    quads = first.shape[0]
    outer, inner = lax.axis_index("outer"), lax.axis_index("inner")
    me = outer * n_inner + inner

    def columns(block, part=0):
        return pl.ds(pl.multiple_of(part * width + block * LANES, LANES), LANES)

    n_z = n_inner // 2
    n_x = n // n_inner // 2
    x, core = lax.div(outer, 2), lax.rem(outer, 2)
    z, y = lax.div(inner, 2), lax.rem(inner, 2)

    def partner(step):
        turn_of = lax.div(step, n_z)
        to_z = lax.rem(z + step + (n_z // 2) * core, n_z)
        to_x = lax.rem(x + turn_of + y, n_x)
        to_y = lax.rem(y + lax.div(turn_of, n_x) + core, 2)
        to_core = lax.rem(core + lax.div(turn_of, 2 * n_x), 2)
        to = (to_x * 2 + to_core, to_z * 2 + to_y)
        return to, to[0] * n_inner + to[1]

    def each_partner(body):
        def run(step, carry):
            to, number = partner(step)

            @pl.when(number != me)
            def _():
                body(to, number)
            return carry
        lax.fori_loop(0, n, run, 0)

    def loop(count, body):
        def run(step, carry):
            body(step)
            return carry
        lax.fori_loop(0, count, run, 0)

    def halo_copy(to):
        return pltpu.make_async_remote_copy(
            src_ref=halo_out, dst_ref=halo_in, send_sem=halo_send, recv_sem=halo_recv,
            device_id=(lax.div(to, n_inner), lax.rem(to, n_inner)), device_id_type=MESH,
        )

    def send(source, target, sems, half, to, number):
        pltpu.make_async_remote_copy(
            src_ref=source.at[half, number], dst_ref=target.at[half, me],
            send_sem=sems.at[0, half], recv_sem=sems.at[1, half],
            device_id=to, device_id_type=MESH,
        ).start()

    def wait_all(buffer, sems, way, half):
        chunks = buffer.at[half, pl.ds(0, n - 1)]
        pltpu.make_async_copy(chunks, chunks, sems.at[way, half]).wait()

    send_filter = functools.partial(send, filt_out, filt_in, f_sems)
    send_gate = functools.partial(send, gate_out, gate_in, g_sems)
    send_conv = functools.partial(send, conv_out, conv_in, y_sems)

    load_tail = pltpu.make_async_copy(
        proj_hbm.at[pl.ds(tok - ROWS, ROWS), :], tail, tail_sem)
    load_tail.start()
    load_filt = pltpu.make_async_copy(filt_hbm, filt, filt_sem)
    load_filt.start()
    load = pltpu.make_async_copy(proj_hbm, proj, proj_sem)
    load.start()

    barrier = pltpu.get_barrier_semaphore()
    each_partner(lambda to, number: pl.semaphore_signal(
        barrier, inc=1, device_id=to, device_id_type=MESH))

    load_tail.wait()
    blocks = proj.shape[1] // LANES
    for block in range(blocks):
        last = tail[:, block * LANES:(block + 1) * LANES].astype(jnp.float32)
        halo[2 * block:2 * block + 2, :] = last[ROWS - 2:]
    halo_out[...] = halo[...].astype(jnp.bfloat16)

    load_filt.wait()
    pl.semaphore_wait(barrier, n - 1)

    @pl.when(me < n - 1)
    def _():
        halo_copy(me + 1).start()

    def packed(values):
        first_half, second_half = swapped_halves(values[:half_tok], values[half_tok:])
        return first_half.astype(jnp.bfloat16), second_half.astype(jnp.bfloat16)

    def pack_filter(block):
        return packed(filt[:, columns(block)].astype(jnp.float32))

    def start_filter(to, number):
        filt_out[0, number], filt_out[1, number] = pack_filter(number)
        send_filter(0, to, number)

    each_partner(start_filter)
    filt_in[0, me], filt_in[1, me] = pack_filter(me)

    load.wait()

    @pl.when(me == 0)
    def _():
        halo[...] = jnp.zeros_like(halo)

    @pl.when(me > 0)
    def _():
        halo_copy(me).wait_recv()
        halo[...] = halo_in[...].astype(jnp.float32)

    upper = lax.broadcasted_iota(jnp.int32, (SUB, LANES), 0) < SUB - 1

    def featured(block, part):
        cols = columns(block, part)
        taps = taps_ref[:, cols].astype(jnp.float32)
        at = 2 * (part * (width // LANES) + block)
        head = jnp.where(upper, halo[pl.ds(at, 1), :], halo[pl.ds(at + 1, 1), :])
        rows = jnp.concatenate([head, proj[:, cols].astype(jnp.float32)], 0)
        total = None
        for tap in range(taps.shape[0]):
            start = SUB - tap
            term = taps[tap:tap + 1] * rows[start:start + tok]
            total = term if total is None else total + term
        return total

    def make_gate(block):
        rounded = (featured(block, 1) * featured(block, 2)).astype(jnp.bfloat16)
        gated[block] = rounded
        return packed(rounded.astype(jnp.float32))

    def start_gate(to, number):
        gate_out[0, number], gate_out[1, number] = make_gate(number)
        send_gate(0, to, number)

    each_partner(start_gate)
    gate_in[0, me], gate_in[1, me] = make_gate(me)
    each_partner(lambda to, number: send_filter(1, to, number))

    left = lax.broadcasted_iota(jnp.int32, (half_tok, LANES), 1) < HALF
    for freq in range(freqs):
        for part in range(2):
            column = turn_ref[part][:, freq:freq + 1]
            turn[freq, part] = jnp.where(left, column[:half_tok], column[half_tok:])
    first[quads - 1] = jnp.zeros(first.shape[1:], first.dtype)

    def spot(tile, shift):
        return pl.ds(pl.multiple_of(shift + tile * ROWS, ROWS), ROWS)

    def pair_lanes(pair):
        return pair // 2, slice((pair % 2) * LANES, (pair % 2 + 1) * LANES)

    def first_section(source, half):
        def run(tile):
            rows = spot(tile, 0)
            spec = forward64([source[half, b, rows, :].astype(jnp.float32) for b in range(n)])

            def turned(freq):
                cos, sin = turn[freq, 0, rows, :], turn[freq, 1, rows, :]
                z = spec[freq]
                if z.im is None:
                    return z.re * cos, -(z.re * sin)
                return z.re * cos + z.im * sin, z.im * cos - z.re * sin

            for pair in range((freqs + 1) // 2):
                even = turned(2 * pair)
                odd = turned(2 * pair + 1) if 2 * pair + 1 < freqs else even
                quad, lanes = pair_lanes(pair)
                for part in range(2):
                    low, high = swapped_halves(even[part], odd[part])
                    first[quad, spot(tile, part * tok), lanes] = low.astype(jnp.bfloat16)
                    first[quad, spot(tile, part * tok + half_tok), lanes] = high.astype(jnp.bfloat16)
        loop(half_tok // ROWS, run)

    def spectrum(quad):
        return jnp.dot(fwd_ref[...], first[quad], preferred_element_type=jnp.float32)

    def filter_section(half):
        first_section(filt_in, half)
        for quad in range(quads):
            fspec[quad] = spectrum(quad)

    def signal_section(half):
        first_section(gate_in, half)
        for quad in range(quads):
            spec = spectrum(quad)
            sr, si = spec[:tok], spec[tok:]
            fr, fi = fspec[quad, :tok], fspec[quad, tok:]
            product = jnp.concatenate([sr * fr - si * fi, sr * fi + si * fr], 0).astype(jnp.bfloat16)
            back[quad] = jnp.dot(bwd_ref[...], product, preferred_element_type=jnp.float32)

    scale = 1.0 / (2 * n * tok)

    def last_section(half):
        def run(tile):
            rows = spot(tile, 0)
            spec = []
            for pair in range((freqs + 1) // 2):
                quad, lanes = pair_lanes(pair)
                parts = [
                    swapped_halves(
                        back[quad, spot(tile, part * tok), lanes],
                        back[quad, spot(tile, part * tok + half_tok), lanes])
                    for part in range(2)
                ]
                for odd in range(2):
                    freq = 2 * pair + odd
                    if freq < freqs:
                        re, im = parts[0][odd], parts[1][odd]
                        cos, sin = turn[freq, 0, rows, :], turn[freq, 1, rows, :]
                        spec.append(Cx(re * cos - im * sin, im * cos + re * sin))
            done = backward64(spec)
            for b in range(n):
                conv_out[half, b, rows, :] = (done[b] * scale).astype(jnp.bfloat16)
        loop(half_tok // ROWS, run)

    wait_all(filt_in, f_sems, 1, 0)
    each_partner(lambda to, number: send_gate(1, to, number))
    filter_section(0)
    wait_all(gate_in, g_sems, 1, 0)
    signal_section(0)
    last_section(0)
    each_partner(lambda to, number: send_conv(0, to, number))
    wait_all(filt_in, f_sems, 1, 1)
    filter_section(1)
    wait_all(gate_in, g_sems, 1, 1)
    signal_section(1)
    last_section(1)
    each_partner(lambda to, number: send_conv(1, to, number))

    def ask(block):
        asked = featured(block, 0)
        query[block] = asked
        direct[block] = asked * (skip_ref[:, columns(block)] * gated[block].astype(jnp.float32))

    loop(n, ask)

    for half in range(2):
        conv_in[half, me] = conv_out[half, me]
        wait_all(conv_in, y_sems, 1, half)

    def finish(block):
        cols = columns(block)
        rows = jnp.concatenate(swapped_halves(
            conv_in[0, block].astype(jnp.float32), conv_in[1, block].astype(jnp.float32)), 0)
        out_ref[:, cols] = (query[block] * rows + direct[block]).astype(jnp.bfloat16)

    loop(n, finish)

    @pl.when(me < n - 1)
    def _():
        halo_copy(me + 1).wait_send()

    for half in range(2):
        wait_all(filt_out, f_sems, 0, half)
        wait_all(gate_out, g_sems, 0, half)
        wait_all(conv_out, y_sems, 0, half)


def cosines(rows, cols, length):
    angle = (np.arange(rows)[:, None] * np.arange(cols)[None, :] % length) * (TWO_PI / length)
    return np.cos(angle), np.sin(angle)


def by_channels(projected, short_filter, long_filter, skip):
    n_inner = lax.axis_size("inner")
    n = lax.axis_size("outer") * n_inner
    tok, width = long_filter.shape
    freqs = n + 1
    cos, sin = cosines(tok, tok, tok)
    forward = np.block([[cos, sin], [-sin, cos]]).astype(jnp.bfloat16)
    backward = np.block([[cos, -sin], [sin, cos]]).astype(jnp.bfloat16)
    turns = np.stack(cosines(tok, LANES, 2 * n * tok)).astype(np.float32)
    vmem = pl.BlockSpec(memory_space=pltpu.VMEM)
    hbm = pl.BlockSpec(memory_space=pl.ANY)
    quads = -(-freqs // 4)
    edges = 2 * projected.shape[1] // LANES
    chunks = pltpu.VMEM((2, n, tok // 2, LANES), jnp.bfloat16)
    dma = pltpu.SemaphoreType.DMA
    return pl.pallas_call(
        functools.partial(kernel, n, n_inner),
        out_shape=jax.ShapeDtypeStruct((tok, width), jnp.bfloat16),
        in_specs=[hbm, hbm] + [vmem] * 5,
        out_specs=vmem,
        scratch_shapes=[
            pltpu.VMEM(projected.shape, jnp.bfloat16),
            pltpu.VMEM(long_filter.shape, jnp.bfloat16),
            pltpu.VMEM((edges, LANES), jnp.float32),
            pltpu.VMEM((edges, LANES), jnp.bfloat16),
            pltpu.VMEM((edges, LANES), jnp.bfloat16),
            chunks, chunks, chunks, chunks, chunks, chunks,
            pltpu.VMEM((n, tok, LANES), jnp.bfloat16),
            pltpu.VMEM((quads, 2 * tok, 4 * HALF), jnp.bfloat16),
            pltpu.VMEM((quads, 2 * tok, 4 * HALF), jnp.float32),
            pltpu.VMEM((quads, 2 * tok, 4 * HALF), jnp.float32),
            pltpu.VMEM((freqs, 2, tok // 2, LANES), jnp.float32),
            pltpu.VMEM((n, tok, LANES), jnp.float32),
            pltpu.VMEM((n, tok, LANES), jnp.float32),
            pltpu.VMEM((ROWS, projected.shape[1]), jnp.bfloat16),
            dma, dma, dma, dma, dma,
            dma((2, 2)), dma((2, 2)), dma((2, 2)),
        ],
        compiler_params=pltpu.CompilerParams(
            collective_id=0, has_side_effects=True, vmem_limit_bytes=56 * 1024 * 1024),
        cost_estimate=pl.CostEstimate(
            flops=2 * 3 * freqs * (2 * tok) ** 2 * LANES,
            bytes_accessed=10 * tok * width, transcendentals=0),
    )(projected, long_filter, short_filter, skip[None, :],
      jnp.asarray(forward), jnp.asarray(backward), jnp.asarray(turns))


def passed_along(value, axis, by):
    length = lax.axis_size(axis)
    pairs = [(i, i + by) for i in range(length) if 0 <= i + by < length]
    return lax.ppermute(value, axis, pairs)


def turn_table(rows, cols, length):
    product = rows * cols % length
    angle = product.astype(jnp.float32) * (TWO_PI / length)
    return (jnp.cos(angle), jnp.sin(angle))


def counting(count):
    return jnp.arange(count, dtype=jnp.int32)


def narrowed(table_pair):
    return (table_pair[0].astype(jnp.bfloat16), table_pair[1].astype(jnp.bfloat16))


def contract(form, table, values):
    return jnp.einsum(form, table, values, preferred_element_type=jnp.float32)


def shards(projected, short_filter, long_filter, skip):
    outer_count = lax.axis_size("outer")
    inner_count = lax.axis_size("inner")
    segments = outer_count * inner_count
    tok_rows, width_cols = long_filter.shape
    local_rows = tok_rows // segments
    freq_rows = 2 * segments
    freq_local = 2
    transform = freq_rows * tok_rows
    position = lax.axis_index(("outer", "inner"))
    tap_count = short_filter.shape[0]
    rim_count = tap_count - 1
    previous_rows = passed_along(projected[tok_rows - rim_count :], ("outer", "inner"), 1)
    extended = jnp.concatenate([previous_rows, projected], 0)
    featured = jnp.zeros(projected.shape, jnp.float32)
    for tap_index in range(tap_count):
        offset = rim_count - tap_index
        featured = featured + short_filter[tap_index].astype(jnp.float32) * extended[
            offset : offset + tok_rows
        ].astype(jnp.float32)
    query_rows = featured[:, :width_cols]
    gated_rows = (featured[:, width_cols : 2 * width_cols] * featured[:, 2 * width_cols :]).astype(
        jnp.bfloat16
    )
    cos_first, sin_first = narrowed(
        turn_table(counting(freq_rows)[:, None], counting(segments)[None, :], freq_rows)
    )
    owned_rows = position * local_rows + counting(local_rows)
    turn_cos, turn_sin = turn_table(counting(freq_rows)[:, None], owned_rows[None, :], transform)
    turn_cos = turn_cos[:, :, None]
    turn_sin = turn_sin[:, :, None]
    cos_local, sin_local = narrowed(
        turn_table(counting(tok_rows)[:, None], counting(tok_rows)[None, :], tok_rows)
    )
    owned_freqs = position * freq_local + counting(freq_local)
    back_cos, back_sin = turn_table(owned_freqs[:, None], counting(tok_rows)[None, :], transform)
    back_cos = back_cos[:, :, None]
    back_sin = back_sin[:, :, None]
    cos_last, sin_last = narrowed(
        turn_table(counting(segments)[:, None], counting(freq_rows)[None, :], freq_rows)
    )

    def first_section(stacked):
        real_part = contract("kb,bac->kac", cos_first, stacked)
        imag_part = -contract("kb,bac->kac", sin_first, stacked)
        out_real = (real_part * turn_cos + imag_part * turn_sin).astype(jnp.bfloat16)
        out_imag = (imag_part * turn_cos - real_part * turn_sin).astype(jnp.bfloat16)
        return (out_real, out_imag)

    def forward_local(real_half, imag_half):
        spec_real = contract("ua,kac->kuc", cos_local, real_half) + contract(
            "ua,kac->kuc", sin_local, imag_half
        )
        spec_imag = contract("ua,kac->kuc", cos_local, imag_half) - contract(
            "ua,kac->kuc", sin_local, real_half
        )
        return (spec_real, spec_imag)

    moved = (
        lax.all_to_all(
            gated_rows.reshape(segments, local_rows, width_cols),
            ("outer", "inner"),
            split_axis=0,
            concat_axis=0,
            tiled=True,
        ),
        lax.all_to_all(
            long_filter.reshape(segments, local_rows, width_cols),
            ("outer", "inner"),
            split_axis=0,
            concat_axis=0,
            tiled=True,
        ),
    )
    signal_cols = moved[0]
    filter_cols = moved[1]
    signal_real, signal_imag = first_section(signal_cols)
    filter_real, filter_imag = first_section(filter_cols)
    spectral_pieces = (
        lax.all_to_all(signal_real, ("outer", "inner"), split_axis=0, concat_axis=1, tiled=True),
        lax.all_to_all(signal_imag, ("outer", "inner"), split_axis=0, concat_axis=1, tiled=True),
        lax.all_to_all(filter_real, ("outer", "inner"), split_axis=0, concat_axis=1, tiled=True),
        lax.all_to_all(filter_imag, ("outer", "inner"), split_axis=0, concat_axis=1, tiled=True),
    )
    signal_real, signal_imag = forward_local(spectral_pieces[0], spectral_pieces[1])
    filter_real, filter_imag = forward_local(spectral_pieces[2], spectral_pieces[3])
    product_real = (signal_real * filter_real - signal_imag * filter_imag).astype(jnp.bfloat16)
    product_imag = (signal_real * filter_imag + signal_imag * filter_real).astype(jnp.bfloat16)
    back_real = contract("au,kuc->kac", cos_local, product_real) - contract(
        "au,kuc->kac", sin_local, product_imag
    )
    back_imag = contract("au,kuc->kac", cos_local, product_imag) + contract(
        "au,kuc->kac", sin_local, product_real
    )
    out_real = (back_real * back_cos - back_imag * back_sin).astype(jnp.bfloat16)
    out_imag = (back_imag * back_cos + back_real * back_sin).astype(jnp.bfloat16)
    moved = (
        lax.all_to_all(out_real, ("outer", "inner"), split_axis=1, concat_axis=0, tiled=True),
        lax.all_to_all(out_imag, ("outer", "inner"), split_axis=1, concat_axis=0, tiled=True),
    )
    rows_real = moved[0]
    rows_imag = moved[1]
    long_conv = (
        contract("bk,kac->bac", cos_last, rows_real) - contract("bk,kac->bac", sin_last, rows_imag)
    ) * (1.0 / transform)
    moved = lax.all_to_all(
        long_conv.astype(jnp.bfloat16), ("outer", "inner"), split_axis=0, concat_axis=0, tiled=True
    )
    conv_rows = moved.reshape(tok_rows, width_cols)
    mixed = query_rows * (
        conv_rows.astype(jnp.float32) + skip[None, :] * gated_rows.astype(jnp.float32)
    )
    return mixed.astype(jnp.bfloat16)


def operator(projected, short_filter, long_filter, skip):
    segments = lax.axis_size("outer") * lax.axis_size("inner")
    tok_rows, width_cols = long_filter.shape
    if 2 * segments == RADIX * RADIX and tok_rows == LANES and width_cols == segments * LANES:
        return by_channels(projected, short_filter, long_filter, skip)
    return shards(projected, short_filter, long_filter, skip)


def solution(mesh):
    in_specs = (P(("outer", "inner"), None), P(), P(("outer", "inner"), None), P())
    out_specs = P(("outer", "inner"), None)
    return jax.shard_map(operator, mesh=mesh, in_specs=in_specs, out_specs=out_specs, check_vma=False)
```

```python
import functools
import math

import jax
import jax.numpy as jnp
import numpy as np
from jax import lax
from jax.experimental import pallas as pl
from jax.experimental.pallas import tpu as pltpu
from jax.sharding import PartitionSpec as P

TWO_PI = 2.0 * math.pi
MESH = pl.DeviceIdType.MESH
LANES = 128
HALF = LANES // 2
ROWS = 16
SUB = 8
RADIX = 8


class Cx:
    def __init__(self, re, im=None):
        self.re, self.im = re, im

    def __add__(self, other):
        if self.im is None:
            im = other.im
        elif other.im is None:
            im = self.im
        else:
            im = self.im + other.im
        return Cx(self.re + other.re, im)

    def __sub__(self, other):
        if other.im is None:
            im = self.im
        elif self.im is None:
            im = -other.im
        else:
            im = self.im - other.im
        return Cx(self.re - other.re, im)

    def conj(self):
        return Cx(self.re, None if self.im is None else -self.im)

    def times(self, turns, length):
        turns = turns % length
        if turns == 0:
            return self
        if 2 * turns == length:
            return Cx(-self.re, None if self.im is None else -self.im)
        cos, sin = math.cos(TWO_PI * turns / length), math.sin(TWO_PI * turns / length)
        if self.im is None:
            return Cx(self.re * cos, self.re * sin)
        if 8 * turns % length == 0 and 4 * turns % length != 0:
            half = math.sqrt(0.5)
            one, two = self.re * half, self.im * half
            signs = (round(cos / half), round(sin / half))
            re = {(1, 1): one - two, (1, -1): one + two, (-1, 1): -(one + two), (-1, -1): two - one}
            im = {(1, 1): one + two, (1, -1): two - one, (-1, 1): one - two, (-1, -1): -(one + two)}
            return Cx(re[signs], im[signs])
        return Cx(self.re * cos - self.im * sin, self.re * sin + self.im * cos)

    def plus_i(self, other, sign):
        if other.im is None:
            re = self.re
        else:
            re = self.re - other.im if sign > 0 else self.re + other.im
        turned = other.re if sign > 0 else -other.re
        return Cx(re, turned if self.im is None else self.im + turned)


def dft4(z, sign):
    s, t, u, v = z[0] + z[2], z[0] - z[2], z[1] + z[3], z[1] - z[3]
    return [s + u, t.plus_i(v, sign), s - u, t.plus_i(v, -sign)]


def dft8(z, sign):
    even, odd = dft4(z[0::2], sign), dft4(z[1::2], sign)
    out = [None] * 8
    for k in range(4):
        if k == 2:
            out[2], out[6] = even[2].plus_i(odd[2], sign), even[2].plus_i(odd[2], -sign)
        else:
            turned = odd[k].times(sign * k, 8)
            out[k], out[k + 4] = even[k] + turned, even[k] - turned
    return out


def forward64(x):
    half = math.sqrt(0.5)
    first = [[None] * 8 for _ in range(5)]
    for b in range(8):
        x0, x1, x2, x3 = x[b], x[b + 8], x[b + 16], x[b + 24]
        p, q, d = x0 + x2, x1 + x3, x1 - x3
        e, f = q * half, d * half
        first[0][b] = Cx(p + q)
        first[4][b] = Cx(p - q)
        first[2][b] = Cx(x0 - x2, -d)
        first[1][b] = Cx(x0 + f, -(e + x2))
        first[3][b] = Cx(x0 - f, x2 - e)
    out = {}
    for k1 in range(5):
        done = dft8([first[k1][b].times(-b * k1, 64) for b in range(8)], -1)
        for k0 in range(8):
            freq = k1 + 8 * k0
            if freq <= 32:
                out[freq] = done[k0]
            elif k1 not in (0, 4):
                out[64 - freq] = done[k0].conj()
    return out


def backward64(spec):
    half = math.sqrt(0.5)
    held = [None] * 5
    for k1 in range(5):
        values = []
        for k0 in range(8):
            freq = k1 + 8 * k0
            values.append(spec[freq] if freq <= 32 else spec[64 - freq].conj())
        done = dft8(values, 1)
        held[k1] = [done[b].times(b * k1, 64) for b in range(8)]
    out = [None] * 32
    for b in range(8):
        h0, h4 = held[0][b].re, held[4][b].re
        h1, h2, h3 = held[1][b], held[2][b], held[3][b]
        plus, minus = h0 + h4, h0 - h4
        a1, a3 = (h1.re - h3.re), (h1.im + h3.im)
        out[b] = plus + 2.0 * (h1.re + h2.re + h3.re)
        out[b + 16] = plus + 2.0 * (h3.im - h1.im - h2.re)
        out[b + 8] = minus + 2.0 * (half * (a1 - a3) - h2.im)
        out[b + 24] = minus + 2.0 * (h2.im - half * (a1 + a3))
    return out


def swapped_halves(x, y):
    left = lax.broadcasted_iota(jnp.int32, x.shape, 1) < HALF
    return (
        jnp.where(left, x, pltpu.roll(y, HALF, 1)),
        jnp.where(left, pltpu.roll(x, HALF, 1), y),
    )


def kernel(
    n, n_inner, proj_hbm, filt_hbm, taps_ref, skip_ref, fwd_ref, bwd_ref, turn_ref, out_ref,
    proj, filt, halo, halo_out, halo_in, filt_out, gate_out, conv_out, filt_in, gate_in, conv_in,
    gated, first, fspec, back, turn, query, direct, tail,
    tail_sem, proj_sem, filt_sem, halo_send, halo_recv, f_sems, g_sems, y_sems,
):
    tok, width = filt.shape
    freqs = n + 1
    half_tok = tok // 2
    quads = first.shape[0]
    outer, inner = lax.axis_index("outer"), lax.axis_index("inner")
    me = outer * n_inner + inner

    def columns(block, part=0):
        return pl.ds(pl.multiple_of(part * width + block * LANES, LANES), LANES)

    n_z = n_inner // 2
    n_x = n // n_inner // 2
    x, core = lax.div(outer, 2), lax.rem(outer, 2)
    z, y = lax.div(inner, 2), lax.rem(inner, 2)

    def partner(step):
        turn_of = lax.div(step, n_z)
        to_z = lax.rem(z + step + (n_z // 2) * core, n_z)
        to_x = lax.rem(x + turn_of + y, n_x)
        to_y = lax.rem(y + lax.div(turn_of, n_x) + core, 2)
        to_core = lax.rem(core + lax.div(turn_of, 2 * n_x), 2)
        to = (to_x * 2 + to_core, to_z * 2 + to_y)
        return to, to[0] * n_inner + to[1]

    def each_partner(body):
        def run(step, carry):
            to, number = partner(step)

            @pl.when(number != me)
            def _():
                body(to, number)
            return carry
        lax.fori_loop(0, n, run, 0)

    def loop(count, body, unroll=1):
        def run(step, carry):
            body(step)
            return carry
        lax.fori_loop(0, count, run, 0, unroll=unroll)

    def halo_copy(to):
        return pltpu.make_async_remote_copy(
            src_ref=halo_out, dst_ref=halo_in, send_sem=halo_send, recv_sem=halo_recv,
            device_id=(lax.div(to, n_inner), lax.rem(to, n_inner)), device_id_type=MESH,
        )

    def send(source, target, sems, half, to, number):
        pltpu.make_async_remote_copy(
            src_ref=source.at[half, number], dst_ref=target.at[half, me],
            send_sem=sems.at[0, half], recv_sem=sems.at[1, half],
            device_id=to, device_id_type=MESH,
        ).start()

    def wait_all(buffer, sems, way, half):
        chunks = buffer.at[half, pl.ds(0, n - 1)]
        pltpu.make_async_copy(chunks, chunks, sems.at[way, half]).wait()

    send_filter = functools.partial(send, filt_out, filt_in, f_sems)
    send_gate = functools.partial(send, gate_out, gate_in, g_sems)
    send_conv = functools.partial(send, conv_out, conv_in, y_sems)

    load_tail = pltpu.make_async_copy(
        proj_hbm.at[pl.ds(tok - ROWS, ROWS), :], tail, tail_sem)
    load_tail.start()
    load_filt = pltpu.make_async_copy(filt_hbm, filt, filt_sem)
    load_filt.start()
    load = pltpu.make_async_copy(proj_hbm, proj, proj_sem)
    load.start()

    barrier = pltpu.get_barrier_semaphore()
    each_partner(lambda to, number: pl.semaphore_signal(
        barrier, inc=1, device_id=to, device_id_type=MESH))

    load_tail.wait()
    blocks = proj.shape[1] // LANES
    for block in range(blocks):
        last = tail[:, block * LANES:(block + 1) * LANES].astype(jnp.float32)
        halo[2 * block:2 * block + 2, :] = last[ROWS - 2:]
    halo_out[...] = halo[...].astype(jnp.bfloat16)

    left = lax.broadcasted_iota(jnp.int32, (half_tok, LANES), 1) < HALF
    for freq in range(freqs):
        for part in range(2):
            column = turn_ref[part][:, freq:freq + 1]
            turn[freq, part] = jnp.where(left, column[:half_tok], column[half_tok:])
    first[quads - 1] = jnp.zeros(first.shape[1:], first.dtype)

    load_filt.wait()
    pl.semaphore_wait(barrier, n - 1)

    @pl.when(me < n - 1)
    def _():
        halo_copy(me + 1).start()

    def packed(values):
        first_half, second_half = swapped_halves(values[:half_tok], values[half_tok:])
        return first_half.astype(jnp.bfloat16), second_half.astype(jnp.bfloat16)

    def pack_filter(block):
        return packed(filt[:, columns(block)].astype(jnp.float32))

    def start_filter(to, number):
        filt_out[0, number], filt_out[1, number] = pack_filter(number)
        send_filter(0, to, number)

    each_partner(start_filter)
    filt_in[0, me], filt_in[1, me] = pack_filter(me)

    load.wait()

    @pl.when(me == 0)
    def _():
        halo[...] = jnp.zeros_like(halo)

    @pl.when(me > 0)
    def _():
        halo_copy(me).wait_recv()
        halo[...] = halo_in[...].astype(jnp.float32)

    upper = lax.broadcasted_iota(jnp.int32, (SUB, LANES), 0) < SUB - 1

    def featured(block, part):
        cols = columns(block, part)
        taps = taps_ref[:, cols].astype(jnp.float32)
        at = 2 * (part * (width // LANES) + block)
        head = jnp.where(upper, halo[pl.ds(at, 1), :], halo[pl.ds(at + 1, 1), :])
        rows = jnp.concatenate([head, proj[:, cols].astype(jnp.float32)], 0)
        total = None
        for tap in range(taps.shape[0]):
            start = SUB - tap
            term = taps[tap:tap + 1] * rows[start:start + tok]
            total = term if total is None else total + term
        return total

    def make_gate(block):
        rounded = (featured(block, 1) * featured(block, 2)).astype(jnp.bfloat16)
        gated[block] = rounded
        return packed(rounded.astype(jnp.float32))

    def start_gate(to, number):
        gate_out[0, number], gate_out[1, number] = make_gate(number)
        send_gate(0, to, number)

    each_partner(start_gate)
    gate_in[0, me], gate_in[1, me] = make_gate(me)
    each_partner(lambda to, number: send_filter(1, to, number))

    def spot(tile, shift):
        return pl.ds(pl.multiple_of(shift + tile * ROWS, ROWS), ROWS)

    def pair_lanes(pair):
        return pair // 2, slice((pair % 2) * LANES, (pair % 2 + 1) * LANES)

    def first_section(source, half):
        def run(tile):
            rows = spot(tile, 0)
            spec = forward64([source[half, b, rows, :].astype(jnp.float32) for b in range(n)])

            def turned(freq):
                cos, sin = turn[freq, 0, rows, :], turn[freq, 1, rows, :]
                z = spec[freq]
                if z.im is None:
                    return z.re * cos, -(z.re * sin)
                return z.re * cos + z.im * sin, z.im * cos - z.re * sin

            for pair in range((freqs + 1) // 2):
                even = turned(2 * pair)
                odd = turned(2 * pair + 1) if 2 * pair + 1 < freqs else even
                quad, lanes = pair_lanes(pair)
                for part in range(2):
                    low, high = swapped_halves(even[part], odd[part])
                    first[quad, spot(tile, part * tok), lanes] = low.astype(jnp.bfloat16)
                    first[quad, spot(tile, part * tok + half_tok), lanes] = high.astype(jnp.bfloat16)
        loop(half_tok // ROWS, run)

    def spectrum(quad):
        return jnp.dot(fwd_ref[...], first[quad], preferred_element_type=jnp.float32)

    def filter_section(half):
        first_section(filt_in, half)
        for quad in range(quads):
            fspec[quad] = spectrum(quad)

    def signal_section(half):
        first_section(gate_in, half)
        for quad in range(quads):
            spec = spectrum(quad)
            sr, si = spec[:tok], spec[tok:]
            fr, fi = fspec[quad, :tok], fspec[quad, tok:]
            product = jnp.concatenate([sr * fr - si * fi, sr * fi + si * fr], 0).astype(jnp.bfloat16)
            back[quad] = jnp.dot(bwd_ref[...], product, preferred_element_type=jnp.float32)

    scale = 1.0 / (2 * n * tok)

    def last_section(half):
        def run(tile):
            rows = spot(tile, 0)
            spec = []
            for pair in range((freqs + 1) // 2):
                quad, lanes = pair_lanes(pair)
                parts = [
                    swapped_halves(
                        back[quad, spot(tile, part * tok), lanes],
                        back[quad, spot(tile, part * tok + half_tok), lanes])
                    for part in range(2)
                ]
                for odd in range(2):
                    freq = 2 * pair + odd
                    if freq < freqs:
                        re, im = parts[0][odd], parts[1][odd]
                        cos, sin = turn[freq, 0, rows, :], turn[freq, 1, rows, :]
                        spec.append(Cx(re * cos - im * sin, im * cos + re * sin))
            done = backward64(spec)
            for b in range(n):
                conv_out[half, b, rows, :] = (done[b] * scale).astype(jnp.bfloat16)
        loop(half_tok // ROWS, run)

    wait_all(filt_in, f_sems, 1, 0)
    each_partner(lambda to, number: send_gate(1, to, number))
    filter_section(0)
    wait_all(gate_in, g_sems, 1, 0)
    signal_section(0)
    last_section(0)
    each_partner(lambda to, number: send_conv(0, to, number))
    wait_all(filt_in, f_sems, 1, 1)
    filter_section(1)
    wait_all(gate_in, g_sems, 1, 1)
    signal_section(1)
    last_section(1)
    each_partner(lambda to, number: send_conv(1, to, number))

    def ask(block):
        asked = featured(block, 0)
        query[block] = asked
        direct[block] = asked * (skip_ref[:, columns(block)] * gated[block].astype(jnp.float32))

    loop(n, ask)

    for half in range(2):
        conv_in[half, me] = conv_out[half, me]
        wait_all(conv_in, y_sems, 1, half)

    def finish(block):
        cols = columns(block)
        rows = jnp.concatenate(swapped_halves(
            conv_in[0, block].astype(jnp.float32), conv_in[1, block].astype(jnp.float32)), 0)
        out_ref[:, cols] = (query[block] * rows + direct[block]).astype(jnp.bfloat16)

    loop(n, finish, unroll=4)

    @pl.when(me < n - 1)
    def _():
        halo_copy(me + 1).wait_send()

    for half in range(2):
        wait_all(filt_out, f_sems, 0, half)
        wait_all(gate_out, g_sems, 0, half)
        wait_all(conv_out, y_sems, 0, half)


def cosines(rows, cols, length):
    angle = (np.arange(rows)[:, None] * np.arange(cols)[None, :] % length) * (TWO_PI / length)
    return np.cos(angle), np.sin(angle)


def by_channels(projected, short_filter, long_filter, skip):
    n_inner = lax.axis_size("inner")
    n = lax.axis_size("outer") * n_inner
    tok, width = long_filter.shape
    freqs = n + 1
    cos, sin = cosines(tok, tok, tok)
    forward = np.block([[cos, sin], [-sin, cos]]).astype(jnp.bfloat16)
    backward = np.block([[cos, -sin], [sin, cos]]).astype(jnp.bfloat16)
    turns = np.stack(cosines(tok, LANES, 2 * n * tok)).astype(np.float32)
    vmem = pl.BlockSpec(memory_space=pltpu.VMEM)
    hbm = pl.BlockSpec(memory_space=pl.ANY)
    quads = -(-freqs // 4)
    edges = 2 * projected.shape[1] // LANES
    chunks = pltpu.VMEM((2, n, tok // 2, LANES), jnp.bfloat16)
    dma = pltpu.SemaphoreType.DMA
    return pl.pallas_call(
        functools.partial(kernel, n, n_inner),
        out_shape=jax.ShapeDtypeStruct((tok, width), jnp.bfloat16),
        in_specs=[hbm, hbm] + [vmem] * 5,
        out_specs=vmem,
        scratch_shapes=[
            pltpu.VMEM(projected.shape, jnp.bfloat16),
            pltpu.VMEM(long_filter.shape, jnp.bfloat16),
            pltpu.VMEM((edges, LANES), jnp.float32),
            pltpu.VMEM((edges, LANES), jnp.bfloat16),
            pltpu.VMEM((edges, LANES), jnp.bfloat16),
            chunks, chunks, chunks, chunks, chunks, chunks,
            pltpu.VMEM((n, tok, LANES), jnp.bfloat16),
            pltpu.VMEM((quads, 2 * tok, 4 * HALF), jnp.bfloat16),
            pltpu.VMEM((quads, 2 * tok, 4 * HALF), jnp.float32),
            pltpu.VMEM((quads, 2 * tok, 4 * HALF), jnp.float32),
            pltpu.VMEM((freqs, 2, tok // 2, LANES), jnp.float32),
            pltpu.VMEM((n, tok, LANES), jnp.float32),
            pltpu.VMEM((n, tok, LANES), jnp.float32),
            pltpu.VMEM((ROWS, projected.shape[1]), jnp.bfloat16),
            dma, dma, dma, dma, dma,
            dma((2, 2)), dma((2, 2)), dma((2, 2)),
        ],
        compiler_params=pltpu.CompilerParams(
            collective_id=0, has_side_effects=True, vmem_limit_bytes=56 * 1024 * 1024),
        cost_estimate=pl.CostEstimate(
            flops=2 * 3 * freqs * (2 * tok) ** 2 * LANES,
            bytes_accessed=10 * tok * width, transcendentals=0),
    )(projected, long_filter, short_filter, skip[None, :],
      jnp.asarray(forward), jnp.asarray(backward), jnp.asarray(turns))


def passed_along(value, axis, by):
    length = lax.axis_size(axis)
    pairs = [(i, i + by) for i in range(length) if 0 <= i + by < length]
    return lax.ppermute(value, axis, pairs)


def turn_table(rows, cols, length):
    product = rows * cols % length
    angle = product.astype(jnp.float32) * (TWO_PI / length)
    return (jnp.cos(angle), jnp.sin(angle))


def counting(count):
    return jnp.arange(count, dtype=jnp.int32)


def narrowed(table_pair):
    return (table_pair[0].astype(jnp.bfloat16), table_pair[1].astype(jnp.bfloat16))


def contract(form, table, values):
    return jnp.einsum(form, table, values, preferred_element_type=jnp.float32)


def shards(projected, short_filter, long_filter, skip):
    outer_count = lax.axis_size("outer")
    inner_count = lax.axis_size("inner")
    segments = outer_count * inner_count
    tok_rows, width_cols = long_filter.shape
    local_rows = tok_rows // segments
    freq_rows = 2 * segments
    freq_local = 2
    transform = freq_rows * tok_rows
    position = lax.axis_index(("outer", "inner"))
    tap_count = short_filter.shape[0]
    rim_count = tap_count - 1
    previous_rows = passed_along(projected[tok_rows - rim_count :], ("outer", "inner"), 1)
    extended = jnp.concatenate([previous_rows, projected], 0)
    featured = jnp.zeros(projected.shape, jnp.float32)
    for tap_index in range(tap_count):
        offset = rim_count - tap_index
        featured = featured + short_filter[tap_index].astype(jnp.float32) * extended[
            offset : offset + tok_rows
        ].astype(jnp.float32)
    query_rows = featured[:, :width_cols]
    gated_rows = (featured[:, width_cols : 2 * width_cols] * featured[:, 2 * width_cols :]).astype(
        jnp.bfloat16
    )
    cos_first, sin_first = narrowed(
        turn_table(counting(freq_rows)[:, None], counting(segments)[None, :], freq_rows)
    )
    owned_rows = position * local_rows + counting(local_rows)
    turn_cos, turn_sin = turn_table(counting(freq_rows)[:, None], owned_rows[None, :], transform)
    turn_cos = turn_cos[:, :, None]
    turn_sin = turn_sin[:, :, None]
    cos_local, sin_local = narrowed(
        turn_table(counting(tok_rows)[:, None], counting(tok_rows)[None, :], tok_rows)
    )
    owned_freqs = position * freq_local + counting(freq_local)
    back_cos, back_sin = turn_table(owned_freqs[:, None], counting(tok_rows)[None, :], transform)
    back_cos = back_cos[:, :, None]
    back_sin = back_sin[:, :, None]
    cos_last, sin_last = narrowed(
        turn_table(counting(segments)[:, None], counting(freq_rows)[None, :], freq_rows)
    )

    def first_section(stacked):
        real_part = contract("kb,bac->kac", cos_first, stacked)
        imag_part = -contract("kb,bac->kac", sin_first, stacked)
        out_real = (real_part * turn_cos + imag_part * turn_sin).astype(jnp.bfloat16)
        out_imag = (imag_part * turn_cos - real_part * turn_sin).astype(jnp.bfloat16)
        return (out_real, out_imag)

    def forward_local(real_half, imag_half):
        spec_real = contract("ua,kac->kuc", cos_local, real_half) + contract(
            "ua,kac->kuc", sin_local, imag_half
        )
        spec_imag = contract("ua,kac->kuc", cos_local, imag_half) - contract(
            "ua,kac->kuc", sin_local, real_half
        )
        return (spec_real, spec_imag)

    moved = (
        lax.all_to_all(
            gated_rows.reshape(segments, local_rows, width_cols),
            ("outer", "inner"),
            split_axis=0,
            concat_axis=0,
            tiled=True,
        ),
        lax.all_to_all(
            long_filter.reshape(segments, local_rows, width_cols),
            ("outer", "inner"),
            split_axis=0,
            concat_axis=0,
            tiled=True,
        ),
    )
    signal_cols = moved[0]
    filter_cols = moved[1]
    signal_real, signal_imag = first_section(signal_cols)
    filter_real, filter_imag = first_section(filter_cols)
    spectral_pieces = (
        lax.all_to_all(signal_real, ("outer", "inner"), split_axis=0, concat_axis=1, tiled=True),
        lax.all_to_all(signal_imag, ("outer", "inner"), split_axis=0, concat_axis=1, tiled=True),
        lax.all_to_all(filter_real, ("outer", "inner"), split_axis=0, concat_axis=1, tiled=True),
        lax.all_to_all(filter_imag, ("outer", "inner"), split_axis=0, concat_axis=1, tiled=True),
    )
    signal_real, signal_imag = forward_local(spectral_pieces[0], spectral_pieces[1])
    filter_real, filter_imag = forward_local(spectral_pieces[2], spectral_pieces[3])
    product_real = (signal_real * filter_real - signal_imag * filter_imag).astype(jnp.bfloat16)
    product_imag = (signal_real * filter_imag + signal_imag * filter_real).astype(jnp.bfloat16)
    back_real = contract("au,kuc->kac", cos_local, product_real) - contract(
        "au,kuc->kac", sin_local, product_imag
    )
    back_imag = contract("au,kuc->kac", cos_local, product_imag) + contract(
        "au,kuc->kac", sin_local, product_real
    )
    out_real = (back_real * back_cos - back_imag * back_sin).astype(jnp.bfloat16)
    out_imag = (back_imag * back_cos + back_real * back_sin).astype(jnp.bfloat16)
    moved = (
        lax.all_to_all(out_real, ("outer", "inner"), split_axis=1, concat_axis=0, tiled=True),
        lax.all_to_all(out_imag, ("outer", "inner"), split_axis=1, concat_axis=0, tiled=True),
    )
    rows_real = moved[0]
    rows_imag = moved[1]
    long_conv = (
        contract("bk,kac->bac", cos_last, rows_real) - contract("bk,kac->bac", sin_last, rows_imag)
    ) * (1.0 / transform)
    moved = lax.all_to_all(
        long_conv.astype(jnp.bfloat16), ("outer", "inner"), split_axis=0, concat_axis=0, tiled=True
    )
    conv_rows = moved.reshape(tok_rows, width_cols)
    mixed = query_rows * (
        conv_rows.astype(jnp.float32) + skip[None, :] * gated_rows.astype(jnp.float32)
    )
    return mixed.astype(jnp.bfloat16)


def operator(projected, short_filter, long_filter, skip):
    segments = lax.axis_size("outer") * lax.axis_size("inner")
    tok_rows, width_cols = long_filter.shape
    if 2 * segments == RADIX * RADIX and tok_rows == LANES and width_cols == segments * LANES:
        return by_channels(projected, short_filter, long_filter, skip)
    return shards(projected, short_filter, long_filter, skip)


def solution(mesh):
    in_specs = (P(("outer", "inner"), None), P(), P(("outer", "inner"), None), P())
    out_specs = P(("outer", "inner"), None)
    return jax.shard_map(operator, mesh=mesh, in_specs=in_specs, out_specs=out_specs, check_vma=False)
```
